32 devices in a mesh: dp: 8 (over z, core), fsdp: 4 (over y, x).
Axes of the slice: x: 2, y: 2, z: 4, core: 2. Of those that a mesh axis runs over, the one named last changes fastest.
Arguments:
- hidden: bfloat16 [8192, 4096], P(('dp', 'fsdp')), may hold values from -6 to 6
- keys: bfloat16 [8192, 512], P(('dp', 'fsdp')), may hold values from -2.5 to 2.5
- queries: bfloat16 [512, 2048], P(('dp', 'fsdp')), may hold values from -2.5 to 2.5
- value_weight: bfloat16 [4096, 512], P('fsdp'), may hold values from -0.09375 to 0.09375
- adapter_down: bfloat16 [4096, 32], P('fsdp'), may hold values from -0.09375 to 0.09375
- adapter_up: bfloat16 [32, 512], replicated, may hold values from -1 to 1
- lengths: int32 [32, 16], P(('dp', 'fsdp')), may hold values from 1 to 32, as said below
- partner: int32 [512], P(('dp', 'fsdp')), may hold values from 0 to 511, as said below
Outputs:
- loss: float32 [], replicated
- adapter_down_grad: float32 [4096, 32], P('fsdp')
- adapter_up_grad: float32 [32, 512], replicated
The draws below stay inside these ranges and needn't reach their ends.
Inputs may be any that keep to these rules, and one draw needn't show every extreme that they name: Each row holds the lengths of one device's 16 strings, laid one after another from its first token row, and they sum to 256. A permutation: partner[i] is the string paired with string i, never i itself.
All inputs are finite; a program needn't handle non-finite values.
Results may differ from the reference program's by a relative error of at most 0.024.
Values may be sent and summed in bfloat16 or wider, within the bound.
A program may use at most 64 MiB of HBM per device.

```python
import math
import jax
import jax.numpy as jnp
from jax import lax

D = 4096
HEADS = 16
KVH = 4
HD = 128
RANK = 32
MAXLEN = 32
TOK_DEV = 256
STR_DEV = 16
EMB = 2048
STRINGS = 512
TOKENS = 8192
N_DP = 8
N_FSDP = 4


def string_lengths(key):
    length_key = jax.random.fold_in(key, 101)
    key_pairs, key_first, key_shuffle = jax.random.split(length_key, 3)
    device_count = TOKENS // TOK_DEV
    mean_len = TOK_DEV // STR_DEV
    shifts = jax.random.randint(key_pairs, (device_count, STR_DEV), -(mean_len - 1), mean_len)
    firsts = jax.random.randint(key_first, (device_count, 1), 1, 3 * mean_len - MAXLEN)
    places = jnp.arange(STR_DEV)
    offset_ids = jnp.maximum(places - 3, 0)
    pair_ids = offset_ids // 2
    parity = 1 - 2 * (offset_ids % 2)
    paired = mean_len + parity[None, :] * shifts[:, pair_ids]
    single = (places == STR_DEV - 1) & ((STR_DEV - 3) % 2 == 1)
    paired = jnp.where(single[None, :], mean_len, paired)
    row_base = jnp.where(places[None, :] == 0, MAXLEN, jnp.where(places[None, :] == 1, firsts, jnp.where(places[None, :] == 2, 3 * mean_len - MAXLEN - firsts, paired)))
    row_keys = jax.random.split(key_shuffle, device_count)

    def shuffle_row(row_key):
        return jax.random.permutation(row_key, STR_DEV)
    shuffles = jax.vmap(shuffle_row)(row_keys)
    return jnp.take_along_axis(row_base, shuffles, axis=1).astype(jnp.int32)


def string_order(key):
    order_key = jax.random.fold_in(key, 202)
    ranking = jax.random.permutation(order_key, STRINGS).astype(jnp.int32)
    inverse = jnp.argsort(ranking, stable=True).astype(jnp.int32)
    return (ranking, inverse)


def draw_hidden(key, part):
    lengths_all = string_lengths(key)
    ranking, inverse = string_order(key)
    key = jax.random.fold_in(key, 3)
    key_center, key_jitter = jax.random.split(key, 2)
    device_count = TOKENS // TOK_DEV
    bounds = jnp.cumsum(lengths_all, axis=1)
    positions = jnp.arange(TOK_DEV)
    slot_ids = jnp.sum((positions[None, :, None] >= bounds[:, None, :]).astype(jnp.int32), axis=2)
    string_ids = (jnp.arange(device_count)[:, None] * STR_DEV + slot_ids).reshape(TOKENS)
    cluster_ids = inverse[string_ids] // 16
    centers = jax.random.truncated_normal(key_center, -4.0, 4.0, (STRINGS // 16, D), jnp.float32)
    jitter = jax.random.truncated_normal(key_jitter, -4.0, 4.0, (TOKENS, D), jnp.float32)
    return (0.55 * centers[cluster_ids] + 0.85 * jitter).astype(jnp.bfloat16)


def draw_lengths(key, part):
    return string_lengths(key)


def draw_partner(key, part):
    ranking, inverse = string_order(key)
    group_start = inverse // 16 * 16
    following = group_start + (inverse - group_start + 1) % 16
    return ranking[following].astype(jnp.int32)


def block_levels(key, shape, shards, least, top_value):
    level, own = 1.0, jax.random.fold_in(key, 6)
    for position, blocks in shards:
        draws = jnp.exp(jax.random.uniform(jax.random.fold_in(own, position), (blocks,), jnp.float32, least / len(shards), top_value / len(shards)))
        level = level * jnp.repeat(draws, shape[position] // blocks).reshape([-1 if axis == position else 1 for axis in range(len(shape))])
    return level


def centred(rng, shape, scale, bound, pieces=(), dtype=jnp.bfloat16):
    array = jax.random.normal(rng, shape, jnp.float32) * scale
    if len(pieces) > 0:
        array = block_levels(rng, shape, pieces, -0.22, 0.18) * array
    return jnp.clip(array, min=-bound, max=bound).astype(dtype)


def setup_inputs(seed: int = 0) -> dict:
    key_list = jax.random.split(jax.random.key(seed), 9)
    hidden = draw_hidden(jax.random.fold_in(key_list[8], 71), 0)
    keys = centred(key_list[1], (TOKENS, KVH * HD), 1.0, 2.5, ((0, 32),))
    queries = centred(key_list[2], (STRINGS, EMB), 1.0, 2.5, ((0, 32),))
    value_weight = centred(key_list[3], (D, KVH * HD), D ** -0.5, 0.09375, ((0, 4),))
    adapter_down = centred(key_list[4], (D, RANK), D ** -0.5, 0.09375, ((0, 4),))
    adapter_up = centred(key_list[5], (RANK, KVH * HD), RANK ** -0.5, 1.0)
    lengths = draw_lengths(jax.random.fold_in(key_list[8], 71), 0)
    partner = draw_partner(jax.random.fold_in(key_list[8], 71), 0)
    return {"hidden": hidden, "keys": keys, "queries": queries, "value_weight": value_weight, "adapter_down": adapter_down, "adapter_up": adapter_up, "lengths": lengths, "partner": partner}


sharpness_divisor = 0.05

def reference(hidden, keys, queries, value_weight, adapter_down, adapter_up, lengths, partner):
    devices = N_DP * N_FSDP
    groups = HEADS // KVH
    block = N_FSDP * STR_DEV
    highest = lax.Precision.HIGHEST
    up_f = adapter_up.astype(jnp.float32)
    low = jnp.dot(hidden, adapter_down, preferred_element_type=jnp.float32)
    value = jnp.dot(hidden, value_weight, preferred_element_type=jnp.float32)
    value = value + jnp.dot(low, up_f, precision=highest)
    ends = jnp.cumsum(lengths, axis=1)
    starts = ends - lengths
    positions = jnp.arange(TOK_DEV)
    member = (positions[None, None, :] >= starts[:, :, None]) & (positions[None, None, :] < ends[:, :, None])
    member = member.astype(jnp.float32)
    query_f = queries.astype(jnp.float32).reshape(devices, STR_DEV, KVH, groups, HD)
    key_f = keys.astype(jnp.float32).reshape(devices, TOK_DEV, KVH, HD)
    scores = jnp.einsum('nskgd,ntkd->nskgt', query_f, key_f, precision=highest) / math.sqrt(HD)
    raw = jnp.exp(scores) * member[:, :, None, None, :]
    probs = raw / lax.optimization_barrier(jnp.sum(raw, axis=-1, keepdims=True))
    value4 = value.reshape(devices, TOK_DEV, KVH, HD)
    pooled = jnp.einsum('nskgt,ntkd->nskgd', probs, value4, precision=highest).reshape(STRINGS, EMB)
    norm = jnp.sqrt(lax.optimization_barrier(jnp.sum(pooled * pooled, axis=-1, keepdims=True)) + 1e-06)
    unit = pooled / norm
    encoded_vectors = unit.astype(jnp.bfloat16)
    emb_grid = encoded_vectors.astype(jnp.float32).reshape(N_DP, N_FSDP, STR_DEV, EMB)
    col_ids = jnp.arange(STRINGS)
    grouped = encoded_vectors.reshape(N_DP, block, EMB)
    partner_rows = partner.reshape(N_DP, block)

    def step(col_acc, inputs):
        sample_count, row_partner, index = inputs
        row_ids = index * block + jnp.arange(block)
        cosine_affinity_matrix = jnp.dot(sample_count, encoded_vectors.T, preferred_element_type=jnp.float32) / sharpness_divisor
        exponentiated_affinity = jnp.exp(cosine_affinity_matrix) * (row_ids[:, None] != col_ids[None, :]).astype(jnp.float32)
        matching_pair_indicator = row_partner[:, None] == col_ids[None, :]
        normalizer_sums = lax.optimization_barrier(jnp.sum(exponentiated_affinity, axis=1))
        positive = lax.optimization_barrier(jnp.sum(jnp.where(matching_pair_indicator, cosine_affinity_matrix, 0.0), axis=1))
        loss_terms = jnp.log(normalizer_sums) - positive
        affinity_derivative = (exponentiated_affinity / normalizer_sums[:, None] - matching_pair_indicator.astype(jnp.float32)) / sharpness_divisor
        affinity_derivative = lax.optimization_barrier(affinity_derivative.astype(jnp.bfloat16)).astype(jnp.float32)
        split = affinity_derivative.reshape(block, N_DP, N_FSDP, STR_DEV)
        row_part = jnp.einsum('rafk,afke->rfe', split, emb_grid, precision=highest)
        row_part = lax.optimization_barrier(row_part.astype(jnp.bfloat16)).astype(jnp.float32)
        row_term = lax.optimization_barrier(jnp.sum(row_part, axis=1))
        col_part = jnp.einsum('rj,re->je', affinity_derivative, sample_count.astype(jnp.float32), precision=highest)
        col_part = lax.optimization_barrier(col_part.astype(jnp.bfloat16)).astype(jnp.float32)
        return (col_acc + col_part, (row_term, loss_terms))
    start_acc = jnp.zeros((STRINGS, EMB), jnp.float32)
    col_acc, (row_terms, loss_terms) = lax.scan(step, start_acc, (grouped, partner_rows, jnp.arange(N_DP)))
    loss = jnp.sum(loss_terms) / STRINGS
    grad_emb = row_terms.reshape(STRINGS, EMB) + col_acc
    grad_pooled = (grad_emb - unit * lax.optimization_barrier(jnp.sum(unit * grad_emb, axis=-1, keepdims=True))) / norm
    grad_split = grad_pooled.reshape(devices, STR_DEV, KVH, groups, HD)
    grad_value = jnp.einsum('nskgt,nskgd->ntkd', probs, grad_split, precision=highest).reshape(TOKENS, KVH * HD)
    up_grad = jnp.dot(low.T, grad_value, precision=highest)
    grad_low = jnp.dot(grad_value, up_f.T, precision=highest).astype(jnp.bfloat16)
    down_grad = jnp.dot(hidden.T, grad_low, preferred_element_type=jnp.float32)
    return (loss, down_grad, up_grad)
```

```python
import functools
import math

import jax
import jax.numpy as jnp
from jax import lax
from jax.experimental import pallas as pl
from jax.experimental.pallas import tpu as pltpu
from jax.sharding import PartitionSpec as P

HEADS = 16
KVH = 4
HD = 128


sharpness_divisor = 0.05


def shards(hidden, keys, queries, value_weight, adapter_down, adapter_up, lengths, partner):
    highest = lax.Precision.HIGHEST
    tok_rows = hidden.shape[0]
    strs = queries.shape[0]
    kv_width = value_weight.shape[1]
    emb_width = queries.shape[1]
    groups = HEADS // KVH
    n_fsdp = lax.axis_size("fsdp")
    n_dp = lax.axis_size("dp")
    columns = hidden
    base = jnp.dot(
        columns,
        lax.all_gather(value_weight, "fsdp", axis=0, tiled=True),
        preferred_element_type=jnp.float32,
    )
    low = jnp.dot(
        columns,
        lax.all_gather(adapter_down, "fsdp", axis=0, tiled=True),
        preferred_element_type=jnp.float32,
    )
    up_f = adapter_up.astype(jnp.float32)
    value = base + jnp.dot(low, up_f, precision=highest)
    length_row = lengths[0]
    ends = jnp.cumsum(length_row)
    starts = ends - length_row
    positions = jnp.arange(tok_rows)
    member = (
        (positions[None, :] >= starts[:, None]) & (positions[None, :] < ends[:, None])
    ).astype(jnp.float32)
    query_split = queries.reshape(strs, KVH, groups, HD)
    key_split = keys.reshape(tok_rows, KVH, HD)
    scores = jnp.einsum(
        "skgd,tkd->skgt", query_split, key_split, preferred_element_type=jnp.float32
    ) / math.sqrt(HD)
    raw = jnp.exp(scores) * member[:, None, None, :]
    probs = raw / jnp.sum(raw, axis=-1, keepdims=True)
    value_split = value.reshape(tok_rows, KVH, HD)
    pooled = jnp.einsum("skgt,tkd->skgd", probs, value_split, precision=highest).reshape(
        strs, emb_width
    )
    norm = jnp.sqrt(jnp.sum(pooled * pooled, axis=-1, keepdims=True) + 1e-06)
    unit = pooled / norm
    encoded_vectors = unit.astype(jnp.bfloat16)
    sample_count, row_partner = (
        lax.all_gather(encoded_vectors, "fsdp", axis=0, tiled=True),
        lax.all_gather(partner, "fsdp", axis=0, tiled=True),
    )
    cols = lax.all_gather(encoded_vectors, "dp", axis=0, tiled=True)
    dp_index = lax.axis_index("dp")
    fsdp_index = lax.axis_index("fsdp")
    row_ids = dp_index * (n_fsdp * strs) + jnp.arange(n_fsdp * strs)
    col_local = jnp.arange(n_dp * strs)
    col_ids = (col_local // strs * n_fsdp + fsdp_index) * strs + col_local % strs
    cosine_affinity_matrix = (
        lax.dot_general(
            sample_count, cols, (((1,), (1,)), ((), ())), preferred_element_type=jnp.float32
        )
        / sharpness_divisor
    )
    exponentiated_affinity = jnp.exp(cosine_affinity_matrix) * (
        row_ids[:, None] != col_ids[None, :]
    ).astype(jnp.float32)
    matching_pair_indicator = row_partner[:, None] == col_ids[None, :]
    normalizer_sums, positive = lax.psum(
        (
            jnp.sum(exponentiated_affinity, axis=1),
            jnp.sum(jnp.where(matching_pair_indicator, cosine_affinity_matrix, 0.0), axis=1),
        ),
        "fsdp",
    )
    own_totals = lax.dynamic_slice_in_dim(normalizer_sums, fsdp_index * strs, strs)
    own_positive = lax.dynamic_slice_in_dim(positive, fsdp_index * strs, strs)
    own_loss = jnp.sum(jnp.log(own_totals) - own_positive)
    affinity_derivative = (
        (
            exponentiated_affinity / normalizer_sums[:, None]
            - matching_pair_indicator.astype(jnp.float32)
        )
        / sharpness_divisor
    ).astype(jnp.bfloat16)
    picked = affinity_derivative
    row_part = lax.psum_scatter(
        jnp.dot(picked, cols, preferred_element_type=jnp.float32).astype(jnp.bfloat16),
        "fsdp",
        scatter_dimension=0,
        tiled=True,
    ).astype(jnp.float32)
    picked = affinity_derivative
    col_part = lax.psum_scatter(
        lax.dot_general(
            picked, sample_count, (((0,), (0,)), ((), ())), preferred_element_type=jnp.float32
        ).astype(jnp.bfloat16),
        "dp",
        scatter_dimension=0,
        tiled=True,
    ).astype(jnp.float32)
    grad_emb = row_part + col_part
    grad_pooled = (grad_emb - unit * jnp.sum(unit * grad_emb, axis=-1, keepdims=True)) / norm
    grad_split = grad_pooled.reshape(strs, KVH, groups, HD)
    grad_value = jnp.einsum("skgt,skgd->tkd", probs, grad_split, precision=highest).reshape(
        tok_rows, kv_width
    )
    up_part = lax.dot_general(low, grad_value, (((0,), (0,)), ((), ())), precision=highest)
    grad_low = lax.dot_general(
        grad_value, up_f, (((1,), (1,)), ((), ())), precision=highest
    ).astype(jnp.bfloat16)
    columns = hidden
    shard = lax.psum_scatter(
        lax.dot_general(
            columns, grad_low, (((0,), (0,)), ((), ())), preferred_element_type=jnp.float32
        ).astype(jnp.bfloat16),
        "fsdp",
        scatter_dimension=0,
        tiled=True,
    )
    down_grad = lax.psum(shard, "dp").astype(jnp.float32)
    up_grad, loss_sum = lax.psum((up_part, own_loss), ("dp", "fsdp"))
    loss = loss_sum / (strs * n_dp * n_fsdp)
    return (loss, down_grad, up_grad)


LANES = 128
MESH = pl.DeviceIdType.MESH
HIGHEST = lax.Precision.HIGHEST


def dot(x, y, cx, cy, precision=None):
    return lax.dot_general(
        x, y, (((cx,), (cy,)), ((), ())), precision=precision, preferred_element_type=jnp.float32
    )


def fits(hidden, keys, queries, value_weight, adapter_down, adapter_up, lengths, partner):
    n_dp, n_fsdp = lax.axis_size("dp"), lax.axis_size("fsdp")
    strings = n_dp * n_fsdp * queries.shape[0]
    rank, width = adapter_up.shape
    return (
        n_fsdp == 4
        and n_dp % 2 == 0
        and strings <= 1024
        and queries.shape[0] == 16
        and (rank // 16) * (width // LANES) == n_dp
        and hidden.shape[1] == n_dp * n_fsdp * LANES
    )


def fused(
    n_dp,
    hidden_ref,
    keys_ref,
    queries_ref,
    weight_ref,
    down_in_ref,
    up_ref,
    len_ref,
    partner_ref,
    loss_ref,
    down_ref,
    up_out_ref,
    w_all,
    acc,
    low_t,
    probs,
    emb_all,
    unit_ref,
    totals,
    msg,
    got1,
    sum1,
    got2,
    sum2,
    got3,
    final,
    send_sem,
    w_sem,
    e_sem,
    g_sem,
):
    f32, bf16 = jnp.float32, jnp.bfloat16
    a, f = lax.axis_index("dp"), lax.axis_index("fsdp")
    nz = n_dp // 2
    z, k = a // 2, a % 2
    other = 1 - k
    xn = f + 1 - 2 * (f % 2)
    yn = (f + 2) % 4
    dn = (xn + 2) % 4
    pair_dev = (z * 2 + other, f)
    x_dev, y_dev, d_dev = (a, xn), (a, yn), (a, dn)
    z_list = [(z + r) % nz for r in range(nz)]
    z_devs = [(zz * 2 + k, f) for zz in z_list]

    barrier = pltpu.get_barrier_semaphore()
    peers = [pair_dev, x_dev, y_dev, d_dev] + z_devs[1:]
    for dev in peers:
        pl.semaphore_signal(barrier, inc=1, device_id=dev, device_id_type=MESH)

    tok, strs = hidden_ref.shape[0], queries_ref.shape[0]
    rank, width = up_ref.shape
    emb_w = queries_ref.shape[1]
    groups = HEADS // KVH
    half = weight_ref.shape[0] // 2
    piece = (half + rank) // 2
    strings = emb_all.shape[0]

    eye = (
        lax.broadcasted_iota(jnp.int32, (rank, rank), 0)
        == lax.broadcasted_iota(jnp.int32, (rank, rank), 1)
    ).astype(bf16)
    for h in range(2):
        w_all[f, h, 0:half, :] = weight_ref[h * half : (h + 1) * half, :]
        w_all[f, h, half : half + rank, :] = dot(
            eye, down_in_ref[h * half : (h + 1) * half, :], 1, 1
        ).astype(bf16)
    pl.semaphore_wait(barrier, len(peers))

    sends = []

    def push(src, dst, recv, dev):
        copy = pltpu.make_async_remote_copy(
            src_ref=src,
            dst_ref=dst,
            send_sem=send_sem.at[len(sends)],
            recv_sem=recv,
            device_id=dev,
            device_id_type=MESH,
        )
        copy.start()
        sends.append(copy)

    def arrive(dst, recv):
        pltpu.make_async_remote_copy(
            src_ref=dst,
            dst_ref=dst,
            send_sem=send_sem.at[0],
            recv_sem=recv,
            device_id=pair_dev,
            device_id_type=MESH,
        ).wait_recv()

    def w_slot(s, h, c):
        return w_all.at[s, h, pl.ds(c * piece, piece), :], w_sem.at[s, h, c]

    def w_push(s, c, dev):
        ref, sem = w_slot(s, k, c)
        push(ref, ref, sem, dev)

    def w_arrive(s, h, c):
        arrive(*w_slot(s, h, c))

    w_push(f, 0, x_dev)
    w_push(f, 1, y_dev)
    w_push(f, 1, x_dev)
    w_push(f, 0, y_dev)

    rows = groups * strs
    row_str = lax.broadcasted_iota(jnp.int32, (rows, strs), 0) % strs
    lane_str = lax.broadcasted_iota(jnp.int32, (rows, strs), 1)
    len_f = jnp.broadcast_to(len_ref[...].astype(f32), (rows, strs))
    ends = jnp.sum(jnp.where(lane_str <= row_str, len_f, 0.0), axis=1, keepdims=True)
    starts = jnp.sum(jnp.where(lane_str < row_str, len_f, 0.0), axis=1, keepdims=True)
    at = lax.broadcasted_iota(jnp.int32, (rows, tok), 1).astype(f32)
    member = (at >= starts) & (at < ends)
    for kv in range(KVH):
        q = jnp.concatenate(
            [
                queries_ref[:, (kv * groups + g) * HD : (kv * groups + g + 1) * HD]
                for g in range(groups)
            ],
            axis=0,
        )
        scores = dot(q, keys_ref[:, kv * HD : (kv + 1) * HD], 1, 1) / math.sqrt(HD)
        raw = jnp.where(member, jnp.exp(scores), 0.0)
        probs[kv] = raw / jnp.sum(raw, axis=1, keepdims=True)

    acc[...] = jnp.zeros_like(acc)
    low_t[...] = jnp.zeros_like(low_t)

    def project(s, h):
        x = hidden_ref[:, pl.ds(pl.multiple_of((2 * s + h) * half, half), half)]
        acc[...] += dot(x, w_all[s, h, 0:half, :], 1, 0)
        low_t[...] += dot(w_all[s, h, half : half + rank, :], x, 1, 1)

    project(f, 0)
    project(f, 1)
    w_arrive(xn, k, 0)
    w_push(xn, 0, y_dev)
    w_push(xn, 0, pair_dev)
    w_arrive(yn, k, 1)
    w_push(yn, 1, x_dev)
    w_push(yn, 1, pair_dev)
    w_arrive(xn, k, 1)
    w_push(xn, 1, pair_dev)
    w_arrive(yn, k, 0)
    w_push(yn, 0, pair_dev)
    project(xn, k)
    project(yn, k)
    for s in (xn, yn):
        for c in range(2):
            w_arrive(s, other, c)
        project(s, other)
    for c in range(2):
        w_arrive(dn, k, c)
        w_push(dn, c, pair_dev)
    project(dn, k)
    for c in range(2):
        w_arrive(dn, other, c)
    project(dn, other)

    up_f = up_ref[...].astype(f32)
    value = acc[...] + dot(low_t[...], up_f, 0, 0, HIGHEST)
    square = jnp.zeros((strs, 1), f32)
    for kv in range(KVH):
        pooled = dot(probs[kv], value[:, kv * HD : (kv + 1) * HD], 1, 0, HIGHEST)
        for g in range(groups):
            part = pooled[g * strs : (g + 1) * strs, :]
            unit_ref[:, (kv * groups + g) * HD : (kv * groups + g + 1) * HD] = part
            square += jnp.sum(part * part, axis=1, keepdims=True)
    norm = jnp.sqrt(square + 1e-06)
    unit = unit_ref[...] / norm
    unit_ref[...] = unit
    emb = unit.astype(bf16)

    def block_of(zz, kk, ff):
        d = (zz * 2 + kk) * 4 + ff
        return emb_all.at[pl.ds(pl.multiple_of(d * strs, strs), strs), :], e_sem.at[d]

    mine = (a * 4 + f) * strs
    own_rows = pl.ds(pl.multiple_of(mine, strs), strs)
    emb_all[own_rows, 0:emb_w] = emb
    partner_row = partner_ref[...].astype(f32)
    own_partner = jnp.sum(
        jnp.where(
            lax.broadcasted_iota(jnp.int32, (strs, strs), 0)
            == lax.broadcasted_iota(jnp.int32, (strs, strs), 1),
            jnp.broadcast_to(partner_row, (strs, strs)),
            0.0,
        ),
        axis=1,
        keepdims=True,
    )
    high = jnp.floor(own_partner * (1.0 / 256.0))
    lane = lax.broadcasted_iota(jnp.int32, (strs, LANES), 1)
    emb_all[own_rows, emb_w : emb_w + LANES] = jnp.where(
        lane == 0, own_partner - 256.0 * high, jnp.where(lane == 1, high, 0.0)
    ).astype(bf16)

    def e_push(blk, dev):
        push(blk[0], blk[0], blk[1], dev)

    own_block = block_of(z, k, f)
    for dev in z_devs[1:]:
        e_push(own_block, dev)
    for dev in (x_dev, y_dev, pair_dev):
        e_push(own_block, dev)
    for r in range(1, nz):
        blk = block_of(z_list[r], k, f)
        arrive(*blk)
        for dev in (x_dev, y_dev, pair_dev):
            e_push(blk, dev)
    for r in range(nz):
        for s, relay in ((xn, y_dev), (yn, x_dev)):
            blk = block_of(z_list[r], k, s)
            arrive(*blk)
            if (r % 2 == 0) == (s is xn):
                e_push(blk, relay)
            e_push(blk, pair_dev)
    for r in range(nz):
        blk = block_of(z_list[r], k, dn)
        arrive(*blk)
        e_push(blk, pair_dev)
    for r in range(nz):
        for s in (f, xn, yn, dn):
            arrive(*block_of(z_list[r], other, s))

    step = min(strings, 128)

    def rows_of(i, loss):
        here = pl.ds(pl.multiple_of(i * step, step), step)
        logits = dot(emb_all[here, 0:emb_w], emb_all[:, 0:emb_w], 1, 1) / sharpness_divisor
        row = i * step + lax.broadcasted_iota(jnp.int32, (step, strings), 0)
        col = lax.broadcasted_iota(jnp.int32, (step, strings), 1)
        total = jnp.sum(jnp.where(row != col, jnp.exp(logits), 0.0), axis=1, keepdims=True)
        totals[here, :] = jnp.broadcast_to(total, (step, LANES))
        code = emb_all[here, emb_w : emb_w + LANES].astype(f32)
        mate = code[:, 0:1] + 256.0 * code[:, 1:2]
        positive = jnp.sum(
            jnp.where(mate == col.astype(f32), logits, 0.0), axis=1, keepdims=True
        )
        return loss + jnp.sum(jnp.log(total) - positive, axis=0, keepdims=True)

    loss = lax.fori_loop(0, strings // step, rows_of, jnp.zeros((1, 1), f32))
    loss_ref[...] = jnp.broadcast_to(loss / strings, loss_ref.shape)

    logits = dot(emb_all[:, 0:emb_w], emb, 1, 1) / sharpness_divisor
    j = lax.broadcasted_iota(jnp.int32, (strings, strs), 0)
    i = mine + lax.broadcasted_iota(jnp.int32, (strings, strs), 1)
    expd = jnp.where(i != j, jnp.exp(logits), 0.0)
    own_total = jnp.sum(expd, axis=0, keepdims=True)
    own_hit = jnp.where(partner_row == j.astype(f32), 1.0, 0.0)
    code = emb_all[:, emb_w : emb_w + LANES].astype(f32)
    mate = code[:, 0:1] + 256.0 * code[:, 1:2]
    hit = jnp.where(mate == i.astype(f32), 1.0, 0.0)
    row_grad = ((expd / own_total - own_hit) / sharpness_divisor).astype(bf16)
    col_grad = ((expd / totals[:, 0:1] - hit) / sharpness_divisor).astype(bf16)
    every = emb_all[:, 0:emb_w]
    grad_emb = dot(row_grad, every, 0, 0) + dot(col_grad, every, 0, 0)
    unit = unit_ref[...]
    grad_pooled = (grad_emb - unit * jnp.sum(unit * grad_emb, axis=1, keepdims=True)) / norm

    for kv in range(KVH):
        g_kv = jnp.concatenate(
            [
                grad_pooled[:, (kv * groups + g) * HD : (kv * groups + g + 1) * HD]
                for g in range(groups)
            ],
            axis=0,
        )
        acc[:, kv * HD : (kv + 1) * HD] = dot(probs[kv], g_kv, 0, 0, HIGHEST)
    grad_value = acc[...]
    up_part = dot(low_t[...], grad_value, 1, 0, HIGHEST).astype(bf16)
    grad_low_t = dot(up_f, grad_value, 1, 1, HIGHEST).astype(bf16)

    per_row = width // LANES
    span = n_dp * LANES
    for ff in range(4):
        part = dot(grad_low_t, hidden_ref[:, ff * span : (ff + 1) * span], 1, 0).astype(bf16)
        for aa in range(n_dp):
            msg[aa % 2, ff, aa // 2, 0:rank, :] = part[:, aa * LANES : (aa + 1) * LANES]
            r0, c0 = aa // per_row * 16, aa % per_row * LANES
            msg[aa % 2, ff, aa // 2, rank : rank + 16, :] = up_part[r0 : r0 + 16, c0 : c0 + LANES]

    push(msg.at[other], got1, g_sem.at[0], pair_dev)
    arrive(got1, g_sem.at[0])
    sum1[...] = (msg[k].astype(f32) + got1[...].astype(f32)).astype(bf16)
    for n, (s, dev) in enumerate(((xn, x_dev), (yn, y_dev), (dn, d_dev))):
        push(sum1.at[s], got2.at[f], g_sem.at[1 + f], dev)
    got2[f] = sum1[f]
    for s in (xn, yn, dn):
        arrive(got2.at[s], g_sem.at[1 + s])
    total2 = got2[0].astype(f32)
    for s in range(1, 4):
        total2 += got2[s].astype(f32)
    sum2[...] = total2.astype(bf16)
    for r in range(1, nz):
        push(sum2.at[z_list[r]], got3.at[z], g_sem.at[5 + z], z_devs[r])
    got3[z] = sum2[z]
    for r in range(1, nz):
        arrive(got3.at[z_list[r]], g_sem.at[5 + z_list[r]])
    total3 = got3[0].astype(f32)
    for s in range(1, nz):
        total3 += got3[s].astype(f32)
    final[k, z] = total3.astype(bf16)
    fin = final.at[k, z]
    base = 5 + nz
    for dev in z_devs[1:] + [pair_dev]:
        push(fin, fin, g_sem.at[base + a], dev)
    for r in range(1, nz):
        slot, sem = final.at[k, z_list[r]], g_sem.at[base + z_list[r] * 2 + k]
        arrive(slot, sem)
        push(slot, slot, sem, pair_dev)
    for r in range(nz):
        arrive(final.at[other, z_list[r]], g_sem.at[base + z_list[r] * 2 + other])
    for aa in range(n_dp):
        r0, c0 = aa // per_row * 16, aa % per_row * LANES
        down_ref[:, aa * LANES : (aa + 1) * LANES] = final[aa % 2, aa // 2, 0:rank, :].astype(f32)
        up_out_ref[r0 : r0 + 16, c0 : c0 + LANES] = final[
            aa % 2, aa // 2, rank : rank + 16, :
        ].astype(f32)
    for copy in sends:
        copy.wait_send()


def fused_shards(hidden, keys, queries, value_weight, adapter_down, adapter_up, lengths, partner):
    n_dp, n_fsdp = lax.axis_size("dp"), lax.axis_size("fsdp")
    tok, depth = hidden.shape
    strs, emb_w = queries.shape
    shard, width = value_weight.shape
    rank = adapter_up.shape[0]
    nz = n_dp // 2
    strings = n_dp * n_fsdp * strs
    f32, bf16 = jnp.float32, jnp.bfloat16
    tall = rank + 16
    vmem = pl.BlockSpec(memory_space=pltpu.VMEM)
    blocks = n_dp * n_fsdp
    loss, down_t, up_grad = pl.pallas_call(
        functools.partial(fused, n_dp),
        out_shape=(
            jax.ShapeDtypeStruct((8, LANES), f32),
            jax.ShapeDtypeStruct((rank, shard), f32),
            jax.ShapeDtypeStruct((rank, width), f32),
        ),
        in_specs=[vmem] * 8,
        out_specs=(vmem,) * 3,
        scratch_shapes=[
            pltpu.VMEM((n_fsdp, 2, shard // 2 + rank, width), bf16),
            pltpu.VMEM((tok, width), f32),
            pltpu.VMEM((rank, tok), f32),
            pltpu.VMEM((KVH, strs * HEADS // KVH, tok), f32),
            pltpu.VMEM((strings, emb_w + LANES), bf16),
            pltpu.VMEM((strs, emb_w), f32),
            pltpu.VMEM((strings, LANES), f32),
            pltpu.VMEM((2, n_fsdp, nz, tall, LANES), bf16),
            pltpu.VMEM((n_fsdp, nz, tall, LANES), bf16),
            pltpu.VMEM((n_fsdp, nz, tall, LANES), bf16),
            pltpu.VMEM((n_fsdp, nz, tall, LANES), bf16),
            pltpu.VMEM((nz, tall, LANES), bf16),
            pltpu.VMEM((nz, tall, LANES), bf16),
            pltpu.VMEM((2, nz, tall, LANES), bf16),
            pltpu.SemaphoreType.DMA((64 + 4 * n_dp,)),
            pltpu.SemaphoreType.DMA((n_fsdp, 2, 2)),
            pltpu.SemaphoreType.DMA((blocks,)),
            pltpu.SemaphoreType.DMA((5 + nz + n_dp,)),
        ],
        compiler_params=pltpu.CompilerParams(
            collective_id=0, has_side_effects=True, vmem_limit_bytes=48 * 1024 * 1024
        ),
    )(
        hidden,
        keys,
        queries,
        value_weight,
        adapter_down,
        adapter_up,
        lengths,
        partner.reshape(1, strs),
    )
    return (loss[0, 0], down_t.T, up_grad)


def solution(mesh):
    placed = (
        P(("dp", "fsdp"), None),
        P(("dp", "fsdp"), None),
        P(("dp", "fsdp"), None),
        P("fsdp", None),
        P("fsdp", None),
        P(),
        P(("dp", "fsdp"), None),
        P(("dp", "fsdp")),
    )

    def body(*args):
        return (fused_shards if fits(*args) else shards)(*args)

    return jax.shard_map(
        body, mesh=mesh, in_specs=placed, out_specs=(P(), P("fsdp", None), P()), check_vma=False
    )
```

```python
import functools
import math

import jax
import jax.numpy as jnp
from jax import lax
from jax.experimental import pallas as pl
from jax.experimental.pallas import tpu as pltpu
from jax.sharding import PartitionSpec as P

HEADS = 16
KVH = 4
HD = 128


sharpness_divisor = 0.05


def shards(hidden, keys, queries, value_weight, adapter_down, adapter_up, lengths, partner):
    highest = lax.Precision.HIGHEST
    tok_rows = hidden.shape[0]
    strs = queries.shape[0]
    kv_width = value_weight.shape[1]
    emb_width = queries.shape[1]
    groups = HEADS // KVH
    n_fsdp = lax.axis_size("fsdp")
    n_dp = lax.axis_size("dp")
    columns = hidden
    base = jnp.dot(
        columns,
        lax.all_gather(value_weight, "fsdp", axis=0, tiled=True),
        preferred_element_type=jnp.float32,
    )
    low = jnp.dot(
        columns,
        lax.all_gather(adapter_down, "fsdp", axis=0, tiled=True),
        preferred_element_type=jnp.float32,
    )
    up_f = adapter_up.astype(jnp.float32)
    value = base + jnp.dot(low, up_f, precision=highest)
    length_row = lengths[0]
    ends = jnp.cumsum(length_row)
    starts = ends - length_row
    positions = jnp.arange(tok_rows)
    member = (
        (positions[None, :] >= starts[:, None]) & (positions[None, :] < ends[:, None])
    ).astype(jnp.float32)
    query_split = queries.reshape(strs, KVH, groups, HD)
    key_split = keys.reshape(tok_rows, KVH, HD)
    scores = jnp.einsum(
        "skgd,tkd->skgt", query_split, key_split, preferred_element_type=jnp.float32
    ) / math.sqrt(HD)
    raw = jnp.exp(scores) * member[:, None, None, :]
    probs = raw / jnp.sum(raw, axis=-1, keepdims=True)
    value_split = value.reshape(tok_rows, KVH, HD)
    pooled = jnp.einsum("skgt,tkd->skgd", probs, value_split, precision=highest).reshape(
        strs, emb_width
    )
    norm = jnp.sqrt(jnp.sum(pooled * pooled, axis=-1, keepdims=True) + 1e-06)
    unit = pooled / norm
    encoded_vectors = unit.astype(jnp.bfloat16)
    sample_count, row_partner = (
        lax.all_gather(encoded_vectors, "fsdp", axis=0, tiled=True),
        lax.all_gather(partner, "fsdp", axis=0, tiled=True),
    )
    cols = lax.all_gather(encoded_vectors, "dp", axis=0, tiled=True)
    dp_index = lax.axis_index("dp")
    fsdp_index = lax.axis_index("fsdp")
    row_ids = dp_index * (n_fsdp * strs) + jnp.arange(n_fsdp * strs)
    col_local = jnp.arange(n_dp * strs)
    col_ids = (col_local // strs * n_fsdp + fsdp_index) * strs + col_local % strs
    cosine_affinity_matrix = (
        lax.dot_general(
            sample_count, cols, (((1,), (1,)), ((), ())), preferred_element_type=jnp.float32
        )
        / sharpness_divisor
    )
    exponentiated_affinity = jnp.exp(cosine_affinity_matrix) * (
        row_ids[:, None] != col_ids[None, :]
    ).astype(jnp.float32)
    matching_pair_indicator = row_partner[:, None] == col_ids[None, :]
    normalizer_sums, positive = lax.psum(
        (
            jnp.sum(exponentiated_affinity, axis=1),
            jnp.sum(jnp.where(matching_pair_indicator, cosine_affinity_matrix, 0.0), axis=1),
        ),
        "fsdp",
    )
    own_totals = lax.dynamic_slice_in_dim(normalizer_sums, fsdp_index * strs, strs)
    own_positive = lax.dynamic_slice_in_dim(positive, fsdp_index * strs, strs)
    own_loss = jnp.sum(jnp.log(own_totals) - own_positive)
    affinity_derivative = (
        (
            exponentiated_affinity / normalizer_sums[:, None]
            - matching_pair_indicator.astype(jnp.float32)
        )
        / sharpness_divisor
    ).astype(jnp.bfloat16)
    picked = affinity_derivative
    row_part = lax.psum_scatter(
        jnp.dot(picked, cols, preferred_element_type=jnp.float32).astype(jnp.bfloat16),
        "fsdp",
        scatter_dimension=0,
        tiled=True,
    ).astype(jnp.float32)
    picked = affinity_derivative
    col_part = lax.psum_scatter(
        lax.dot_general(
            picked, sample_count, (((0,), (0,)), ((), ())), preferred_element_type=jnp.float32
        ).astype(jnp.bfloat16),
        "dp",
        scatter_dimension=0,
        tiled=True,
    ).astype(jnp.float32)
    grad_emb = row_part + col_part
    grad_pooled = (grad_emb - unit * jnp.sum(unit * grad_emb, axis=-1, keepdims=True)) / norm
    grad_split = grad_pooled.reshape(strs, KVH, groups, HD)
    grad_value = jnp.einsum("skgt,skgd->tkd", probs, grad_split, precision=highest).reshape(
        tok_rows, kv_width
    )
    up_part = lax.dot_general(low, grad_value, (((0,), (0,)), ((), ())), precision=highest)
    grad_low = lax.dot_general(
        grad_value, up_f, (((1,), (1,)), ((), ())), precision=highest
    ).astype(jnp.bfloat16)
    columns = hidden
    shard = lax.psum_scatter(
        lax.dot_general(
            columns, grad_low, (((0,), (0,)), ((), ())), preferred_element_type=jnp.float32
        ).astype(jnp.bfloat16),
        "fsdp",
        scatter_dimension=0,
        tiled=True,
    )
    down_grad = lax.psum(shard, "dp").astype(jnp.float32)
    up_grad, loss_sum = lax.psum((up_part, own_loss), ("dp", "fsdp"))
    loss = loss_sum / (strs * n_dp * n_fsdp)
    return (loss, down_grad, up_grad)


LANES = 128
MESH = pl.DeviceIdType.MESH
HIGHEST = lax.Precision.HIGHEST


def dot(x, y, cx, cy, precision=None):
    return lax.dot_general(
        x, y, (((cx,), (cy,)), ((), ())), precision=precision, preferred_element_type=jnp.float32
    )


def fits(hidden, keys, queries, value_weight, adapter_down, adapter_up, lengths, partner):
    n_dp, n_fsdp = lax.axis_size("dp"), lax.axis_size("fsdp")
    strings = n_dp * n_fsdp * queries.shape[0]
    rank, width = adapter_up.shape
    return (
        n_fsdp == 4
        and n_dp % 2 == 0
        and strings <= 1024
        and queries.shape[0] == 16
        and (rank // 16) * (width // LANES) == n_dp
        and hidden.shape[1] == n_dp * n_fsdp * LANES
    )


def fused(
    n_dp,
    hidden_hbm,
    keys_hbm,
    queries_hbm,
    weight_hbm,
    down_in_hbm,
    up_hbm,
    len_hbm,
    partner_hbm,
    loss_ref,
    down_ref,
    up_out_ref,
    hidden_ref,
    keys_ref,
    queries_ref,
    up_ref,
    len_ref,
    partner_ref,
    w_all,
    acc,
    low_t,
    probs,
    emb_all,
    unit_ref,
    totals,
    msg,
    got1,
    sum1,
    got2,
    sum2,
    got3,
    final,
    send_sem,
    w_sem,
    e_sem,
    g_sem,
    load_sem,
):
    f32, bf16 = jnp.float32, jnp.bfloat16
    a, f = lax.axis_index("dp"), lax.axis_index("fsdp")
    nz = n_dp // 2
    z, k = a // 2, a % 2
    other = 1 - k
    xn = f + 1 - 2 * (f % 2)
    yn = (f + 2) % 4
    dn = (xn + 2) % 4
    pair_dev = (z * 2 + other, f)
    x_dev, y_dev, d_dev = (a, xn), (a, yn), (a, dn)
    z_list = [(z + r) % nz for r in range(nz)]
    z_devs = [(zz * 2 + k, f) for zz in z_list]

    barrier = pltpu.get_barrier_semaphore()
    peers = [pair_dev, x_dev, y_dev, d_dev] + z_devs[1:]
    for dev in peers:
        pl.semaphore_signal(barrier, inc=1, device_id=dev, device_id_type=MESH)

    tok, strs = hidden_ref.shape[0], queries_ref.shape[0]
    rank, width = up_ref.shape
    emb_w = queries_ref.shape[1]
    groups = HEADS // KVH
    half = weight_hbm.shape[0] // 2
    tall = half + rank
    edge = tall // 4 // 16 * 16
    sizes = [edge, tall // 2 - edge, tall // 2 - edge, edge]
    offsets = [0, edge, tall // 2, tall - edge]
    strings = emb_all.shape[0]

    loads = []

    def load(src, dst):
        copy = pltpu.make_async_copy(src, dst, load_sem.at[len(loads)])
        copy.start()
        loads.append(copy)

    for h in range(2):
        load(weight_hbm.at[pl.ds(h * half, half), :], w_all.at[f, h, pl.ds(0, half), :])
        load(down_in_hbm.at[:, pl.ds(h * half, half)], w_all.at[f, h, pl.ds(half, rank), :])
    load(queries_hbm, queries_ref)
    load(keys_hbm, keys_ref)
    load(len_hbm, len_ref)
    load(partner_hbm, partner_ref)
    load(up_hbm, up_ref)
    load(hidden_hbm, hidden_ref)
    for copy in loads[:4]:
        copy.wait()
    pl.semaphore_wait(barrier, len(peers))

    sends = []

    def push(src, dst, recv, dev):
        copy = pltpu.make_async_remote_copy(
            src_ref=src,
            dst_ref=dst,
            send_sem=send_sem.at[len(sends)],
            recv_sem=recv,
            device_id=dev,
            device_id_type=MESH,
        )
        copy.start()
        sends.append(copy)

    def arrive(dst, recv):
        pltpu.make_async_remote_copy(
            src_ref=dst,
            dst_ref=dst,
            send_sem=send_sem.at[0],
            recv_sem=recv,
            device_id=pair_dev,
            device_id_type=MESH,
        ).wait_recv()

    flip = z % 2
    z_dev = ((z + 1 - 2 * flip) * 2 + k, f)

    def w_slot(s, h, q):
        start = offsets[q] + flip * (offsets[3 - q] - offsets[q])
        here = pl.ds(pl.multiple_of(start, 16), sizes[q])
        return w_all.at[s, h, here, :], w_sem.at[s, h, q + flip * (3 - 2 * q)]

    def w_push(s, q, dev):
        ref, sem = w_slot(s, k, q)
        push(ref, ref, sem, dev)

    def w_arrive(s, h, q):
        arrive(*w_slot(s, h, q))

    for q in range(3):
        w_push(f, q, x_dev)
        w_push(f, (1, 0, 2)[q], y_dev)
    for copy in loads[4:]:
        copy.wait()

    rows = groups * strs
    row_str = lax.broadcasted_iota(jnp.int32, (rows, strs), 0) % strs
    lane_str = lax.broadcasted_iota(jnp.int32, (rows, strs), 1)
    len_f = jnp.broadcast_to(len_ref[...].astype(f32), (rows, strs))
    ends = jnp.sum(jnp.where(lane_str <= row_str, len_f, 0.0), axis=1, keepdims=True)
    starts = jnp.sum(jnp.where(lane_str < row_str, len_f, 0.0), axis=1, keepdims=True)
    at = lax.broadcasted_iota(jnp.int32, (rows, tok), 1).astype(f32)
    member = (at >= starts) & (at < ends)
    for kv in range(KVH):
        q = jnp.concatenate(
            [
                queries_ref[:, (kv * groups + g) * HD : (kv * groups + g + 1) * HD]
                for g in range(groups)
            ],
            axis=0,
        )
        scores = dot(q, keys_ref[:, kv * HD : (kv + 1) * HD], 1, 1) / math.sqrt(HD)
        raw = jnp.where(member, jnp.exp(scores), 0.0)
        probs[kv] = raw / jnp.sum(raw, axis=1, keepdims=True)

    acc[...] = jnp.zeros_like(acc)
    low_t[...] = jnp.zeros_like(low_t)

    def project(s, h):
        x = hidden_ref[:, pl.ds(pl.multiple_of((2 * s + h) * half, half), half)]
        acc[...] += dot(x, w_all[s, h, 0:half, :], 1, 0)
        low_t[...] += dot(w_all[s, h, half : half + rank, :], x, 1, 1)

    project(f, 0)
    project(f, 1)
    for s, q, on in (
        (xn, 0, (y_dev, z_dev)),
        (yn, 1, (x_dev,)),
        (yn, 0, (z_dev,)),
        (xn, 1, ()),
        (xn, 2, ()),
        (yn, 2, ()),
        (xn, 3, ()),
        (yn, 3, ()),
    ):
        w_arrive(s, k, q)
        for dev in on:
            w_push(s, q, dev)
        w_push(s, q, pair_dev)
    project(xn, k)
    project(yn, k)
    for q in (0, 1):
        w_arrive(dn, k, q)
        w_push(dn, q, z_dev)
        w_push(dn, q, pair_dev)
    for s in (xn, yn):
        for q in range(4):
            w_arrive(s, other, q)
        project(s, other)
    for q in (3, 2):
        w_arrive(dn, k, q)
        w_push(dn, q, pair_dev)
    project(dn, k)
    for q in range(4):
        w_arrive(dn, other, q)
    project(dn, other)
    up_f = up_ref[...].astype(f32)
    value = acc[...] + dot(low_t[...], up_f, 0, 0, HIGHEST)
    square = jnp.zeros((strs, 1), f32)
    for kv in range(KVH):
        pooled = dot(probs[kv], value[:, kv * HD : (kv + 1) * HD], 1, 0, HIGHEST)
        for g in range(groups):
            part = pooled[g * strs : (g + 1) * strs, :]
            unit_ref[:, (kv * groups + g) * HD : (kv * groups + g + 1) * HD] = part
            square += jnp.sum(part * part, axis=1, keepdims=True)
    norm = jnp.sqrt(square + 1e-06)
    unit = unit_ref[...] / norm
    unit_ref[...] = unit
    emb = unit.astype(bf16)

    def block_of(zz, kk, ff):
        d = (zz * 2 + kk) * 4 + ff
        return emb_all.at[pl.ds(pl.multiple_of(d * strs, strs), strs), :], e_sem.at[d]

    mine = (a * 4 + f) * strs
    own_rows = pl.ds(pl.multiple_of(mine, strs), strs)
    emb_all[own_rows, 0:emb_w] = emb
    partner_row = partner_ref[...].astype(f32)
    own_partner = jnp.sum(
        jnp.where(
            lax.broadcasted_iota(jnp.int32, (strs, strs), 0)
            == lax.broadcasted_iota(jnp.int32, (strs, strs), 1),
            jnp.broadcast_to(partner_row, (strs, strs)),
            0.0,
        ),
        axis=1,
        keepdims=True,
    )
    high = jnp.floor(own_partner * (1.0 / 256.0))
    lane = lax.broadcasted_iota(jnp.int32, (strs, LANES), 1)
    emb_all[own_rows, emb_w : emb_w + LANES] = jnp.where(
        lane == 0, own_partner - 256.0 * high, jnp.where(lane == 1, high, 0.0)
    ).astype(bf16)

    def e_push(blk, dev):
        push(blk[0], blk[0], blk[1], dev)

    own_block = block_of(z, k, f)
    for dev in z_devs[1:]:
        e_push(own_block, dev)
    for dev in (x_dev, y_dev, pair_dev):
        e_push(own_block, dev)
    for r in range(1, nz):
        blk = block_of(z_list[r], k, f)
        arrive(*blk)
        for dev in (x_dev, y_dev, pair_dev):
            e_push(blk, dev)
    for r in range(nz):
        for s, relay in ((xn, y_dev), (yn, x_dev)):
            blk = block_of(z_list[r], k, s)
            arrive(*blk)
            if (r % 2 == 0) == (s is xn):
                e_push(blk, relay)
            e_push(blk, pair_dev)
    for r in range(nz):
        blk = block_of(z_list[r], k, dn)
        arrive(*blk)
        e_push(blk, pair_dev)
    for r in range(nz):
        for s in (f, xn, yn, dn):
            arrive(*block_of(z_list[r], other, s))

    step = min(strings, 128)

    def rows_of(i, loss):
        here = pl.ds(pl.multiple_of(i * step, step), step)
        logits = dot(emb_all[here, 0:emb_w], emb_all[:, 0:emb_w], 1, 1) / sharpness_divisor
        row = i * step + lax.broadcasted_iota(jnp.int32, (step, strings), 0)
        col = lax.broadcasted_iota(jnp.int32, (step, strings), 1)
        total = jnp.sum(jnp.where(row != col, jnp.exp(logits), 0.0), axis=1, keepdims=True)
        totals[here, :] = jnp.broadcast_to(total, (step, LANES))
        code = emb_all[here, emb_w : emb_w + LANES].astype(f32)
        mate = code[:, 0:1] + 256.0 * code[:, 1:2]
        positive = jnp.sum(
            jnp.where(mate == col.astype(f32), logits, 0.0), axis=1, keepdims=True
        )
        return loss + jnp.sum(jnp.log(total) - positive, axis=0, keepdims=True)

    loss = lax.fori_loop(0, strings // step, rows_of, jnp.zeros((1, 1), f32))
    loss_ref[...] = jnp.broadcast_to(loss / strings, loss_ref.shape)

    logits = dot(emb_all[:, 0:emb_w], emb, 1, 1) / sharpness_divisor
    j = lax.broadcasted_iota(jnp.int32, (strings, strs), 0)
    i = mine + lax.broadcasted_iota(jnp.int32, (strings, strs), 1)
    expd = jnp.where(i != j, jnp.exp(logits), 0.0)
    own_total = jnp.sum(expd, axis=0, keepdims=True)
    own_hit = jnp.where(partner_row == j.astype(f32), 1.0, 0.0)
    code = emb_all[:, emb_w : emb_w + LANES].astype(f32)
    mate = code[:, 0:1] + 256.0 * code[:, 1:2]
    hit = jnp.where(mate == i.astype(f32), 1.0, 0.0)
    row_grad = ((expd / own_total - own_hit) / sharpness_divisor).astype(bf16)
    col_grad = ((expd / totals[:, 0:1] - hit) / sharpness_divisor).astype(bf16)
    every = emb_all[:, 0:emb_w]
    grad_emb = dot(row_grad, every, 0, 0) + dot(col_grad, every, 0, 0)
    unit = unit_ref[...]
    grad_pooled = (grad_emb - unit * jnp.sum(unit * grad_emb, axis=1, keepdims=True)) / norm

    for kv in range(KVH):
        g_kv = jnp.concatenate(
            [
                grad_pooled[:, (kv * groups + g) * HD : (kv * groups + g + 1) * HD]
                for g in range(groups)
            ],
            axis=0,
        )
        acc[:, kv * HD : (kv + 1) * HD] = dot(probs[kv], g_kv, 0, 0, HIGHEST)
    grad_value = acc[...]
    up_part = dot(low_t[...], grad_value, 1, 0, HIGHEST).astype(bf16)
    grad_low_t = dot(up_f, grad_value, 1, 1, HIGHEST).astype(bf16)

    per_row = width // LANES
    span = n_dp * LANES
    for ff in range(4):
        part = dot(grad_low_t, hidden_ref[:, ff * span : (ff + 1) * span], 1, 0).astype(bf16)
        for aa in range(n_dp):
            msg[aa % 2, ff, aa // 2, 0:rank, :] = part[:, aa * LANES : (aa + 1) * LANES]
            r0, c0 = aa // per_row * 16, aa % per_row * LANES
            msg[aa % 2, ff, aa // 2, rank : rank + 16, :] = up_part[r0 : r0 + 16, c0 : c0 + LANES]

    push(msg.at[other], got1, g_sem.at[0], pair_dev)
    arrive(got1, g_sem.at[0])
    sum1[...] = (msg[k].astype(f32) + got1[...].astype(f32)).astype(bf16)
    for n, (s, dev) in enumerate(((xn, x_dev), (yn, y_dev), (dn, d_dev))):
        push(sum1.at[s], got2.at[f], g_sem.at[1 + f], dev)
    got2[f] = sum1[f]
    for s in (xn, yn, dn):
        arrive(got2.at[s], g_sem.at[1 + s])
    total2 = got2[0].astype(f32)
    for s in range(1, 4):
        total2 += got2[s].astype(f32)
    sum2[...] = total2.astype(bf16)
    for r in range(1, nz):
        push(sum2.at[z_list[r]], got3.at[z], g_sem.at[5 + z], z_devs[r])
    got3[z] = sum2[z]
    for r in range(1, nz):
        arrive(got3.at[z_list[r]], g_sem.at[5 + z_list[r]])
    total3 = got3[0].astype(f32)
    for s in range(1, nz):
        total3 += got3[s].astype(f32)
    final[k, z] = total3.astype(bf16)
    fin = final.at[k, z]
    base = 5 + nz
    for dev in z_devs[1:] + [pair_dev]:
        push(fin, fin, g_sem.at[base + a], dev)
    for r in range(1, nz):
        slot, sem = final.at[k, z_list[r]], g_sem.at[base + z_list[r] * 2 + k]
        arrive(slot, sem)
        push(slot, slot, sem, pair_dev)
    for r in range(nz):
        arrive(final.at[other, z_list[r]], g_sem.at[base + z_list[r] * 2 + other])
    for aa in range(n_dp):
        r0, c0 = aa // per_row * 16, aa % per_row * LANES
        down_ref[:, aa * LANES : (aa + 1) * LANES] = final[aa % 2, aa // 2, 0:rank, :].astype(f32)
        up_out_ref[r0 : r0 + 16, c0 : c0 + LANES] = final[
            aa % 2, aa // 2, rank : rank + 16, :
        ].astype(f32)
    for copy in sends:
        copy.wait_send()


def fused_shards(hidden, keys, queries, value_weight, adapter_down, adapter_up, lengths, partner):
    n_dp, n_fsdp = lax.axis_size("dp"), lax.axis_size("fsdp")
    tok, depth = hidden.shape
    strs, emb_w = queries.shape
    shard, width = value_weight.shape
    rank = adapter_up.shape[0]
    nz = n_dp // 2
    strings = n_dp * n_fsdp * strs
    f32, bf16 = jnp.float32, jnp.bfloat16
    tall = rank + 16
    vmem = pl.BlockSpec(memory_space=pltpu.VMEM)
    hbm = pl.BlockSpec(memory_space=pltpu.HBM)
    blocks = n_dp * n_fsdp
    loss, down_t, up_grad = pl.pallas_call(
        functools.partial(fused, n_dp),
        out_shape=(
            jax.ShapeDtypeStruct((1, 1), f32),
            jax.ShapeDtypeStruct((rank, shard), f32),
            jax.ShapeDtypeStruct((rank, width), f32),
        ),
        in_specs=[hbm] * 8,
        out_specs=(vmem,) * 3,
        scratch_shapes=[
            pltpu.VMEM(hidden.shape, bf16),
            pltpu.VMEM(keys.shape, bf16),
            pltpu.VMEM(queries.shape, bf16),
            pltpu.VMEM(adapter_up.shape, bf16),
            pltpu.VMEM((1, strs), jnp.int32),
            pltpu.VMEM((1, strs), jnp.int32),
            pltpu.VMEM((n_fsdp, 2, shard // 2 + rank, width), bf16),
            pltpu.VMEM((tok, width), f32),
            pltpu.VMEM((rank, tok), f32),
            pltpu.VMEM((KVH, strs * HEADS // KVH, tok), f32),
            pltpu.VMEM((strings, emb_w + LANES), bf16),
            pltpu.VMEM((strs, emb_w), f32),
            pltpu.VMEM((strings, LANES), f32),
            pltpu.VMEM((2, n_fsdp, nz, tall, LANES), bf16),
            pltpu.VMEM((n_fsdp, nz, tall, LANES), bf16),
            pltpu.VMEM((n_fsdp, nz, tall, LANES), bf16),
            pltpu.VMEM((n_fsdp, nz, tall, LANES), bf16),
            pltpu.VMEM((nz, tall, LANES), bf16),
            pltpu.VMEM((nz, tall, LANES), bf16),
            pltpu.VMEM((2, nz, tall, LANES), bf16),
            pltpu.SemaphoreType.DMA((64 + 4 * n_dp,)),
            pltpu.SemaphoreType.DMA((n_fsdp, 2, 4)),
            pltpu.SemaphoreType.DMA((blocks,)),
            pltpu.SemaphoreType.DMA((5 + nz + n_dp,)),
            pltpu.SemaphoreType.DMA((10,)),
        ],
        compiler_params=pltpu.CompilerParams(
            collective_id=0, has_side_effects=True, vmem_limit_bytes=63 * 1024 * 1024
        ),
    )(
        hidden,
        keys,
        queries,
        value_weight,
        adapter_down.T,
        adapter_up,
        lengths,
        partner.reshape(1, strs),
    )
    return (loss[0, 0], down_t.T, up_grad)


def solution(mesh):
    placed = (
        P(("dp", "fsdp"), None),
        P(("dp", "fsdp"), None),
        P(("dp", "fsdp"), None),
        P("fsdp", None),
        P("fsdp", None),
        P(),
        P(("dp", "fsdp"), None),
        P(("dp", "fsdp")),
    )

    def body(*args):
        return (fused_shards if fits(*args) else shards)(*args)

    return jax.shard_map(
        body, mesh=mesh, in_specs=placed, out_specs=(P(), P("fsdp", None), P()), check_vma=False
    )
```

```python
import functools
import math

import jax
import jax.numpy as jnp
from jax import lax
from jax.experimental import pallas as pl
from jax.experimental.pallas import tpu as pltpu
from jax.sharding import PartitionSpec as P

HEADS = 16
KVH = 4
HD = 128


sharpness_divisor = 0.05


def shards(hidden, keys, queries, value_weight, adapter_down, adapter_up, lengths, partner):
    highest = lax.Precision.HIGHEST
    tok_rows = hidden.shape[0]
    strs = queries.shape[0]
    kv_width = value_weight.shape[1]
    emb_width = queries.shape[1]
    groups = HEADS // KVH
    n_fsdp = lax.axis_size("fsdp")
    n_dp = lax.axis_size("dp")
    columns = hidden
    base = jnp.dot(
        columns,
        lax.all_gather(value_weight, "fsdp", axis=0, tiled=True),
        preferred_element_type=jnp.float32,
    )
    low = jnp.dot(
        columns,
        lax.all_gather(adapter_down, "fsdp", axis=0, tiled=True),
        preferred_element_type=jnp.float32,
    )
    up_f = adapter_up.astype(jnp.float32)
    value = base + jnp.dot(low, up_f, precision=highest)
    length_row = lengths[0]
    ends = jnp.cumsum(length_row)
    starts = ends - length_row
    positions = jnp.arange(tok_rows)
    member = (
        (positions[None, :] >= starts[:, None]) & (positions[None, :] < ends[:, None])
    ).astype(jnp.float32)
    query_split = queries.reshape(strs, KVH, groups, HD)
    key_split = keys.reshape(tok_rows, KVH, HD)
    scores = jnp.einsum(
        "skgd,tkd->skgt", query_split, key_split, preferred_element_type=jnp.float32
    ) / math.sqrt(HD)
    raw = jnp.exp(scores) * member[:, None, None, :]
    probs = raw / jnp.sum(raw, axis=-1, keepdims=True)
    value_split = value.reshape(tok_rows, KVH, HD)
    pooled = jnp.einsum("skgt,tkd->skgd", probs, value_split, precision=highest).reshape(
        strs, emb_width
    )
    norm = jnp.sqrt(jnp.sum(pooled * pooled, axis=-1, keepdims=True) + 1e-06)
    unit = pooled / norm
    encoded_vectors = unit.astype(jnp.bfloat16)
    sample_count, row_partner = (
        lax.all_gather(encoded_vectors, "fsdp", axis=0, tiled=True),
        lax.all_gather(partner, "fsdp", axis=0, tiled=True),
    )
    cols = lax.all_gather(encoded_vectors, "dp", axis=0, tiled=True)
    dp_index = lax.axis_index("dp")
    fsdp_index = lax.axis_index("fsdp")
    row_ids = dp_index * (n_fsdp * strs) + jnp.arange(n_fsdp * strs)
    col_local = jnp.arange(n_dp * strs)
    col_ids = (col_local // strs * n_fsdp + fsdp_index) * strs + col_local % strs
    cosine_affinity_matrix = (
        lax.dot_general(
            sample_count, cols, (((1,), (1,)), ((), ())), preferred_element_type=jnp.float32
        )
        / sharpness_divisor
    )
    exponentiated_affinity = jnp.exp(cosine_affinity_matrix) * (
        row_ids[:, None] != col_ids[None, :]
    ).astype(jnp.float32)
    matching_pair_indicator = row_partner[:, None] == col_ids[None, :]
    normalizer_sums, positive = lax.psum(
        (
            jnp.sum(exponentiated_affinity, axis=1),
            jnp.sum(jnp.where(matching_pair_indicator, cosine_affinity_matrix, 0.0), axis=1),
        ),
        "fsdp",
    )
    own_totals = lax.dynamic_slice_in_dim(normalizer_sums, fsdp_index * strs, strs)
    own_positive = lax.dynamic_slice_in_dim(positive, fsdp_index * strs, strs)
    own_loss = jnp.sum(jnp.log(own_totals) - own_positive)
    affinity_derivative = (
        (
            exponentiated_affinity / normalizer_sums[:, None]
            - matching_pair_indicator.astype(jnp.float32)
        )
        / sharpness_divisor
    ).astype(jnp.bfloat16)
    picked = affinity_derivative
    row_part = lax.psum_scatter(
        jnp.dot(picked, cols, preferred_element_type=jnp.float32).astype(jnp.bfloat16),
        "fsdp",
        scatter_dimension=0,
        tiled=True,
    ).astype(jnp.float32)
    picked = affinity_derivative
    col_part = lax.psum_scatter(
        lax.dot_general(
            picked, sample_count, (((0,), (0,)), ((), ())), preferred_element_type=jnp.float32
        ).astype(jnp.bfloat16),
        "dp",
        scatter_dimension=0,
        tiled=True,
    ).astype(jnp.float32)
    grad_emb = row_part + col_part
    grad_pooled = (grad_emb - unit * jnp.sum(unit * grad_emb, axis=-1, keepdims=True)) / norm
    grad_split = grad_pooled.reshape(strs, KVH, groups, HD)
    grad_value = jnp.einsum("skgt,skgd->tkd", probs, grad_split, precision=highest).reshape(
        tok_rows, kv_width
    )
    up_part = lax.dot_general(low, grad_value, (((0,), (0,)), ((), ())), precision=highest)
    grad_low = lax.dot_general(
        grad_value, up_f, (((1,), (1,)), ((), ())), precision=highest
    ).astype(jnp.bfloat16)
    columns = hidden
    shard = lax.psum_scatter(
        lax.dot_general(
            columns, grad_low, (((0,), (0,)), ((), ())), preferred_element_type=jnp.float32
        ).astype(jnp.bfloat16),
        "fsdp",
        scatter_dimension=0,
        tiled=True,
    )
    down_grad = lax.psum(shard, "dp").astype(jnp.float32)
    up_grad, loss_sum = lax.psum((up_part, own_loss), ("dp", "fsdp"))
    loss = loss_sum / (strs * n_dp * n_fsdp)
    return (loss, down_grad, up_grad)


LANES = 128
MESH = pl.DeviceIdType.MESH
HIGHEST = lax.Precision.HIGHEST


def dot(x, y, cx, cy, precision=None):
    return lax.dot_general(
        x, y, (((cx,), (cy,)), ((), ())), precision=precision, preferred_element_type=jnp.float32
    )


def fits(hidden, keys, queries, value_weight, adapter_down, adapter_up, lengths, partner):
    n_dp, n_fsdp = lax.axis_size("dp"), lax.axis_size("fsdp")
    strings = n_dp * n_fsdp * queries.shape[0]
    rank, width = adapter_up.shape
    return (
        n_fsdp == 4
        and n_dp == 8
        and strings <= 1024
        and queries.shape[0] == 16
        and (rank // 16) * (width // LANES) == n_dp
        and hidden.shape[1] == n_dp * n_fsdp * LANES
    )


def fused(
    n_dp,
    hidden_hbm,
    keys_hbm,
    queries_hbm,
    weight_hbm,
    down_in_hbm,
    up_hbm,
    len_hbm,
    partner_hbm,
    loss_ref,
    down_ref,
    up_out_ref,
    hidden_ref,
    keys_ref,
    queries_ref,
    up_ref,
    len_ref,
    partner_ref,
    w_all,
    acc,
    low_t,
    probs,
    emb_all,
    unit_ref,
    totals,
    msg,
    got1,
    sum1,
    got2,
    sum2,
    got3,
    final,
    send_sem,
    w_sem,
    e_sem,
    g_sem,
    load_sem,
):
    f32, bf16 = jnp.float32, jnp.bfloat16
    a, f = lax.axis_index("dp"), lax.axis_index("fsdp")
    nz = n_dp // 2
    z, k = a // 2, a % 2
    other = 1 - k
    xn = f + 1 - 2 * (f % 2)
    yn = (f + 2) % 4
    dn = (xn + 2) % 4
    pair_dev = (z * 2 + other, f)
    x_dev, y_dev, d_dev = (a, xn), (a, yn), (a, dn)
    upper = z // 2
    inner = z + upper * (3 - 2 * z)
    z_list = [z] + [t + upper * (3 - 2 * t) for t in (1 - inner, 2, 3)]
    z_devs = [(zz * 2 + k, f) for zz in z_list]

    barrier = pltpu.get_barrier_semaphore()
    peers = [pair_dev, x_dev, y_dev, d_dev] + z_devs[1:]
    for dev in peers:
        pl.semaphore_signal(barrier, inc=1, device_id=dev, device_id_type=MESH)

    tok, strs = hidden_ref.shape[0], queries_ref.shape[0]
    rank, width = up_ref.shape
    emb_w = queries_ref.shape[1]
    groups = HEADS // KVH
    half = weight_hbm.shape[0] // 2
    tall = half + rank
    edge = tall // 4 // 16 * 16
    sizes = [edge, tall // 2 - edge, tall // 2 - edge, edge]
    offsets = [0, edge, tall // 2, tall - edge]
    strings = emb_all.shape[0]

    loads = []

    def load(src, dst):
        copy = pltpu.make_async_copy(src, dst, load_sem.at[len(loads)])
        copy.start()
        loads.append(copy)

    for h in range(2):
        load(weight_hbm.at[pl.ds(h * half, half), :], w_all.at[f, h, pl.ds(0, half), :])
        load(down_in_hbm.at[:, pl.ds(h * half, half)], w_all.at[f, h, pl.ds(half, rank), :])
    load(queries_hbm, queries_ref)
    load(keys_hbm, keys_ref)
    load(len_hbm, len_ref)
    load(partner_hbm, partner_ref)
    load(up_hbm, up_ref)
    load(hidden_hbm, hidden_ref)
    for copy in loads[:4]:
        copy.wait()
    pl.semaphore_wait(barrier, len(peers))

    sends = []

    def push(src, dst, recv, dev):
        copy = pltpu.make_async_remote_copy(
            src_ref=src,
            dst_ref=dst,
            send_sem=send_sem.at[len(sends)],
            recv_sem=recv,
            device_id=dev,
            device_id_type=MESH,
        )
        copy.start()
        sends.append(copy)

    drained = []

    def drain():
        for copy in sends[len(drained) :]:
            copy.wait_send()
            drained.append(copy)

    def arrive(dst, recv):
        pltpu.make_async_remote_copy(
            src_ref=dst,
            dst_ref=dst,
            send_sem=send_sem.at[0],
            recv_sem=recv,
            device_id=pair_dev,
            device_id_type=MESH,
        ).wait_recv()

    flip = z % 2
    z_dev = ((z + 1 - 2 * flip) * 2 + k, f)

    def w_slot(s, h, q):
        start = offsets[q] + flip * (offsets[3 - q] - offsets[q])
        here = pl.ds(pl.multiple_of(start, 16), sizes[q])
        return w_all.at[s, h, here, :], w_sem.at[s, h, q + flip * (3 - 2 * q)]

    def w_push(s, q, dev):
        ref, sem = w_slot(s, k, q)
        push(ref, ref, sem, dev)

    def w_arrive(s, h, q):
        arrive(*w_slot(s, h, q))

    for q in range(2):
        w_push(f, q, x_dev)
        w_push(f, 1 - q, y_dev)
    for copy in loads[4:]:
        copy.wait()

    rows = groups * strs
    row_str = lax.broadcasted_iota(jnp.int32, (rows, strs), 0) % strs
    lane_str = lax.broadcasted_iota(jnp.int32, (rows, strs), 1)
    len_f = jnp.broadcast_to(len_ref[...].astype(f32), (rows, strs))
    ends = jnp.sum(jnp.where(lane_str <= row_str, len_f, 0.0), axis=1, keepdims=True)
    starts = jnp.sum(jnp.where(lane_str < row_str, len_f, 0.0), axis=1, keepdims=True)
    at = lax.broadcasted_iota(jnp.int32, (rows, tok), 1).astype(f32)
    member = (at >= starts) & (at < ends)
    for kv in range(KVH):
        q = jnp.concatenate(
            [
                queries_ref[:, (kv * groups + g) * HD : (kv * groups + g + 1) * HD]
                for g in range(groups)
            ],
            axis=0,
        )
        scores = dot(q, keys_ref[:, kv * HD : (kv + 1) * HD], 1, 1) / math.sqrt(HD)
        raw = jnp.where(member, jnp.exp(scores), 0.0)
        probs[kv] = raw / jnp.sum(raw, axis=1, keepdims=True)

    acc[...] = jnp.zeros_like(acc)
    low_t[...] = jnp.zeros_like(low_t)

    def project(s, h):
        x = hidden_ref[:, pl.ds(pl.multiple_of((2 * s + h) * half, half), half)]
        acc[...] += dot(x, w_all[s, h, 0:half, :], 1, 0)
        low_t[...] += dot(w_all[s, h, half : half + rank, :], x, 1, 1)

    project(f, 0)
    project(f, 1)
    def w_relay(s, q, on):
        w_arrive(s, k, q)
        for dev in on:
            w_push(s, q, dev)
        w_push(s, q, pair_dev)

    w_relay(xn, 0, (y_dev, z_dev))
    w_relay(yn, 1, (x_dev,))
    w_push(f, 2, x_dev)
    w_push(f, 2, y_dev)
    w_relay(yn, 0, (z_dev,))
    w_relay(xn, 1, ())
    w_relay(dn, 0, (z_dev,))
    w_relay(dn, 1, (z_dev,))
    for q in (3, 2):
        w_relay(xn, q, ())
        w_relay(yn, q, ())
    project(xn, k)
    project(yn, k)
    for s in (xn, yn):
        for q in range(4):
            w_arrive(s, other, q)
        project(s, other)
    for q in (3, 2):
        w_relay(dn, q, ())
    project(dn, k)
    for q in range(4):
        w_arrive(dn, other, q)
    project(dn, other)
    up_f = up_ref[...].astype(f32)
    value = acc[...] + dot(low_t[...], up_f, 0, 0, HIGHEST)
    square = jnp.zeros((strs, 1), f32)
    for kv in range(KVH):
        pooled = dot(probs[kv], value[:, kv * HD : (kv + 1) * HD], 1, 0, HIGHEST)
        for g in range(groups):
            part = pooled[g * strs : (g + 1) * strs, :]
            unit_ref[:, (kv * groups + g) * HD : (kv * groups + g + 1) * HD] = part
            square += jnp.sum(part * part, axis=1, keepdims=True)
    norm = jnp.sqrt(square + 1e-06)
    unit = unit_ref[...] / norm
    unit_ref[...] = unit
    emb = unit.astype(bf16)

    def block_of(zz, kk, ff):
        d = (zz * 2 + kk) * 4 + ff
        return emb_all.at[pl.ds(pl.multiple_of(d * strs, strs), strs), :], e_sem.at[d]

    mine = (a * 4 + f) * strs
    own_rows = pl.ds(pl.multiple_of(mine, strs), strs)
    emb_all[own_rows, 0:emb_w] = emb
    partner_row = partner_ref[...].astype(f32)
    own_partner = jnp.sum(
        jnp.where(
            lax.broadcasted_iota(jnp.int32, (strs, strs), 0)
            == lax.broadcasted_iota(jnp.int32, (strs, strs), 1),
            jnp.broadcast_to(partner_row, (strs, strs)),
            0.0,
        ),
        axis=1,
        keepdims=True,
    )
    high = jnp.floor(own_partner * (1.0 / 256.0))
    lane = lax.broadcasted_iota(jnp.int32, (strs, LANES), 1)
    emb_all[own_rows, emb_w : emb_w + LANES] = jnp.where(
        lane == 0, own_partner - 256.0 * high, jnp.where(lane == 1, high, 0.0)
    ).astype(bf16)

    def e_push(blk, dev):
        push(blk[0], blk[0], blk[1], dev)

    own_block = block_of(z, k, f)
    for dev in z_devs[1:]:
        e_push(own_block, dev)
    for dev in (x_dev, y_dev, pair_dev):
        e_push(own_block, dev)
    drain()

    def from_z(r, devs):
        blk = block_of(z_list[r], k, f)
        arrive(*blk)
        for dev in devs:
            e_push(blk, dev)

    def from_plane(r):
        for s, relay in ((xn, y_dev), (yn, x_dev)):
            blk = block_of(z_list[r], k, s)
            arrive(*blk)
            if r < nz - 1 and (r % 2 == 0) == (s is xn):
                e_push(blk, relay)
            e_push(blk, pair_dev)

    from_z(1, (x_dev, y_dev, pair_dev))
    from_plane(0)
    from_z(2, (x_dev, y_dev, pair_dev))
    from_plane(1)
    from_z(3, (d_dev, x_dev, y_dev, pair_dev))
    from_plane(2)
    from_plane(3)
    for r in range(nz):
        blk = block_of(z_list[r], k, dn)
        arrive(*blk)
        e_push(blk, pair_dev)
    for r in range(nz):
        for s in (f, xn, yn, dn):
            arrive(*block_of(z_list[r], other, s))

    step = min(strings, 128)

    def rows_of(i, loss):
        here = pl.ds(pl.multiple_of(i * step, step), step)
        logits = dot(emb_all[here, 0:emb_w], emb_all[:, 0:emb_w], 1, 1) * (1.0 / sharpness_divisor)
        row = i * step + lax.broadcasted_iota(jnp.int32, (step, strings), 0)
        col = lax.broadcasted_iota(jnp.int32, (step, strings), 1)
        total = jnp.sum(jnp.where(row != col, jnp.exp(logits), 0.0), axis=1, keepdims=True)
        totals[here, :] = jnp.broadcast_to(total, (step, LANES))
        code = emb_all[here, emb_w : emb_w + LANES].astype(f32)
        mate = code[:, 0:1] + 256.0 * code[:, 1:2]
        positive = jnp.sum(
            jnp.where(mate == col.astype(f32), logits, 0.0), axis=1, keepdims=True
        )
        return loss + jnp.sum(jnp.log(total) - positive, axis=0, keepdims=True)

    loss = lax.fori_loop(0, strings // step, rows_of, jnp.zeros((1, 1), f32))
    loss_ref[...] = jnp.broadcast_to(loss / strings, loss_ref.shape)

    logits = dot(emb_all[:, 0:emb_w], emb, 1, 1) * (1.0 / sharpness_divisor)
    j = lax.broadcasted_iota(jnp.int32, (strings, strs), 0)
    i = mine + lax.broadcasted_iota(jnp.int32, (strings, strs), 1)
    expd = jnp.where(i != j, jnp.exp(logits), 0.0)
    own_total = jnp.sum(expd, axis=0, keepdims=True)
    own_hit = jnp.where(partner_row == j.astype(f32), 1.0, 0.0)
    code = emb_all[:, emb_w : emb_w + LANES].astype(f32)
    mate = code[:, 0:1] + 256.0 * code[:, 1:2]
    hit = jnp.where(mate == i.astype(f32), 1.0, 0.0)
    row_grad = ((expd / own_total - own_hit) * (1.0 / sharpness_divisor)).astype(bf16)
    col_grad = ((expd / totals[:, 0:1] - hit) * (1.0 / sharpness_divisor)).astype(bf16)
    every = emb_all[:, 0:emb_w]
    grad_emb = dot(row_grad, every, 0, 0) + dot(col_grad, every, 0, 0)
    unit = unit_ref[...]
    grad_pooled = (grad_emb - unit * jnp.sum(unit * grad_emb, axis=1, keepdims=True)) / norm

    for kv in range(KVH):
        g_kv = jnp.concatenate(
            [
                grad_pooled[:, (kv * groups + g) * HD : (kv * groups + g + 1) * HD]
                for g in range(groups)
            ],
            axis=0,
        )
        acc[:, kv * HD : (kv + 1) * HD] = dot(probs[kv], g_kv, 0, 0, HIGHEST)
    grad_value = acc[...]
    up_part = dot(low_t[...], grad_value, 1, 0, HIGHEST).astype(bf16)
    grad_low_t = dot(up_f, grad_value, 1, 1, HIGHEST).astype(bf16)

    per_row = width // LANES
    span = n_dp * LANES
    for ff in range(4):
        part = dot(grad_low_t, hidden_ref[:, ff * span : (ff + 1) * span], 1, 0).astype(bf16)
        for aa in range(n_dp):
            msg[aa % 2, ff, aa // 2, 0:rank, :] = part[:, aa * LANES : (aa + 1) * LANES]
            r0, c0 = aa // per_row * 16, aa % per_row * LANES
            msg[aa % 2, ff, aa // 2, rank : rank + 16, :] = up_part[r0 : r0 + 16, c0 : c0 + LANES]

    push(msg.at[other], got1, g_sem.at[0], pair_dev)
    drain()
    arrive(got1, g_sem.at[0])
    sum1[...] = (msg[k].astype(f32) + got1[...].astype(f32)).astype(bf16)
    for n, (s, dev) in enumerate(((xn, x_dev), (yn, y_dev), (dn, d_dev))):
        push(sum1.at[s], got2.at[f], g_sem.at[1 + f], dev)
    got2[f] = sum1[f]
    for s in (xn, yn, dn):
        arrive(got2.at[s], g_sem.at[1 + s])
    total2 = got2[0].astype(f32)
    for s in range(1, 4):
        total2 += got2[s].astype(f32)
    sum2[...] = total2.astype(bf16)
    for r in range(1, nz):
        push(sum2.at[z_list[r]], got3.at[z], g_sem.at[5 + z], z_devs[r])
    got3[z] = sum2[z]
    for r in range(1, nz):
        arrive(got3.at[z_list[r]], g_sem.at[5 + z_list[r]])
    total3 = got3[0].astype(f32)
    for s in range(1, nz):
        total3 += got3[s].astype(f32)
    final[k, z] = total3.astype(bf16)
    fin = final.at[k, z]
    base = 5 + nz
    for dev in z_devs[1:] + [pair_dev]:
        push(fin, fin, g_sem.at[base + a], dev)
    for r in range(1, nz):
        slot, sem = final.at[k, z_list[r]], g_sem.at[base + z_list[r] * 2 + k]
        arrive(slot, sem)
        push(slot, slot, sem, pair_dev)
    for r in range(nz):
        arrive(final.at[other, z_list[r]], g_sem.at[base + z_list[r] * 2 + other])
    for aa in range(n_dp):
        r0, c0 = aa // per_row * 16, aa % per_row * LANES
        down_ref[:, aa * LANES : (aa + 1) * LANES] = final[aa % 2, aa // 2, 0:rank, :].astype(f32)
        up_out_ref[r0 : r0 + 16, c0 : c0 + LANES] = final[
            aa % 2, aa // 2, rank : rank + 16, :
        ].astype(f32)
    drain()


def fused_shards(hidden, keys, queries, value_weight, adapter_down, adapter_up, lengths, partner):
    n_dp, n_fsdp = lax.axis_size("dp"), lax.axis_size("fsdp")
    tok, depth = hidden.shape
    strs, emb_w = queries.shape
    shard, width = value_weight.shape
    rank = adapter_up.shape[0]
    nz = n_dp // 2
    strings = n_dp * n_fsdp * strs
    f32, bf16 = jnp.float32, jnp.bfloat16
    tall = rank + 16
    vmem = pl.BlockSpec(memory_space=pltpu.VMEM)
    hbm = pl.BlockSpec(memory_space=pltpu.HBM)
    blocks = n_dp * n_fsdp
    loss, down_t, up_grad = pl.pallas_call(
        functools.partial(fused, n_dp),
        out_shape=(
            jax.ShapeDtypeStruct((1, 1), f32),
            jax.ShapeDtypeStruct((rank, shard), f32),
            jax.ShapeDtypeStruct((rank, width), f32),
        ),
        in_specs=[hbm] * 8,
        out_specs=(vmem,) * 3,
        scratch_shapes=[
            pltpu.VMEM(hidden.shape, bf16),
            pltpu.VMEM(keys.shape, bf16),
            pltpu.VMEM(queries.shape, bf16),
            pltpu.VMEM(adapter_up.shape, bf16),
            pltpu.VMEM((1, strs), jnp.int32),
            pltpu.VMEM((1, strs), jnp.int32),
            pltpu.VMEM((n_fsdp, 2, shard // 2 + rank, width), bf16),
            pltpu.VMEM((tok, width), f32),
            pltpu.VMEM((rank, tok), f32),
            pltpu.VMEM((KVH, strs * HEADS // KVH, tok), f32),
            pltpu.VMEM((strings, emb_w + LANES), bf16),
            pltpu.VMEM((strs, emb_w), f32),
            pltpu.VMEM((strings, LANES), f32),
            pltpu.VMEM((2, n_fsdp, nz, tall, LANES), bf16),
            pltpu.VMEM((n_fsdp, nz, tall, LANES), bf16),
            pltpu.VMEM((n_fsdp, nz, tall, LANES), bf16),
            pltpu.VMEM((n_fsdp, nz, tall, LANES), bf16),
            pltpu.VMEM((nz, tall, LANES), bf16),
            pltpu.VMEM((nz, tall, LANES), bf16),
            pltpu.VMEM((2, nz, tall, LANES), bf16),
            pltpu.SemaphoreType.DMA((64 + 4 * n_dp,)),
            pltpu.SemaphoreType.DMA((n_fsdp, 2, 4)),
            pltpu.SemaphoreType.DMA((blocks,)),
            pltpu.SemaphoreType.DMA((5 + nz + n_dp,)),
            pltpu.SemaphoreType.DMA((10,)),
        ],
        compiler_params=pltpu.CompilerParams(
            collective_id=0, has_side_effects=True, vmem_limit_bytes=63 * 1024 * 1024
        ),
    )(
        hidden,
        keys,
        queries,
        value_weight,
        adapter_down.T,
        adapter_up,
        lengths,
        partner.reshape(1, strs),
    )
    return (loss[0, 0], down_t.T, up_grad)


def solution(mesh):
    placed = (
        P(("dp", "fsdp"), None),
        P(("dp", "fsdp"), None),
        P(("dp", "fsdp"), None),
        P("fsdp", None),
        P("fsdp", None),
        P(),
        P(("dp", "fsdp"), None),
        P(("dp", "fsdp")),
    )

    def body(*args):
        return (fused_shards if fits(*args) else shards)(*args)

    return jax.shard_map(
        body, mesh=mesh, in_specs=placed, out_specs=(P(), P("fsdp", None), P()), check_vma=False
    )
```

```python
import functools
import math

import jax
import jax.numpy as jnp
from jax import lax
from jax.experimental import pallas as pl
from jax.experimental.pallas import tpu as pltpu
from jax.sharding import PartitionSpec as P

HEADS = 16
KVH = 4
HD = 128


sharpness_divisor = 0.05


def shards(hidden, keys, queries, value_weight, adapter_down, adapter_up, lengths, partner):
    highest = lax.Precision.HIGHEST
    tok_rows = hidden.shape[0]
    strs = queries.shape[0]
    kv_width = value_weight.shape[1]
    emb_width = queries.shape[1]
    groups = HEADS // KVH
    n_fsdp = lax.axis_size("fsdp")
    n_dp = lax.axis_size("dp")
    columns = hidden
    base = jnp.dot(
        columns,
        lax.all_gather(value_weight, "fsdp", axis=0, tiled=True),
        preferred_element_type=jnp.float32,
    )
    low = jnp.dot(
        columns,
        lax.all_gather(adapter_down, "fsdp", axis=0, tiled=True),
        preferred_element_type=jnp.float32,
    )
    up_f = adapter_up.astype(jnp.float32)
    value = base + jnp.dot(low, up_f, precision=highest)
    length_row = lengths[0]
    ends = jnp.cumsum(length_row)
    starts = ends - length_row
    positions = jnp.arange(tok_rows)
    member = (
        (positions[None, :] >= starts[:, None]) & (positions[None, :] < ends[:, None])
    ).astype(jnp.float32)
    query_split = queries.reshape(strs, KVH, groups, HD)
    key_split = keys.reshape(tok_rows, KVH, HD)
    scores = jnp.einsum(
        "skgd,tkd->skgt", query_split, key_split, preferred_element_type=jnp.float32
    ) / math.sqrt(HD)
    raw = jnp.exp(scores) * member[:, None, None, :]
    probs = raw / jnp.sum(raw, axis=-1, keepdims=True)
    value_split = value.reshape(tok_rows, KVH, HD)
    pooled = jnp.einsum("skgt,tkd->skgd", probs, value_split, precision=highest).reshape(
        strs, emb_width
    )
    norm = jnp.sqrt(jnp.sum(pooled * pooled, axis=-1, keepdims=True) + 1e-06)
    unit = pooled / norm
    encoded_vectors = unit.astype(jnp.bfloat16)
    sample_count, row_partner = (
        lax.all_gather(encoded_vectors, "fsdp", axis=0, tiled=True),
        lax.all_gather(partner, "fsdp", axis=0, tiled=True),
    )
    cols = lax.all_gather(encoded_vectors, "dp", axis=0, tiled=True)
    dp_index = lax.axis_index("dp")
    fsdp_index = lax.axis_index("fsdp")
    row_ids = dp_index * (n_fsdp * strs) + jnp.arange(n_fsdp * strs)
    col_local = jnp.arange(n_dp * strs)
    col_ids = (col_local // strs * n_fsdp + fsdp_index) * strs + col_local % strs
    cosine_affinity_matrix = (
        lax.dot_general(
            sample_count, cols, (((1,), (1,)), ((), ())), preferred_element_type=jnp.float32
        )
        / sharpness_divisor
    )
    exponentiated_affinity = jnp.exp(cosine_affinity_matrix) * (
        row_ids[:, None] != col_ids[None, :]
    ).astype(jnp.float32)
    matching_pair_indicator = row_partner[:, None] == col_ids[None, :]
    normalizer_sums, positive = lax.psum(
        (
            jnp.sum(exponentiated_affinity, axis=1),
            jnp.sum(jnp.where(matching_pair_indicator, cosine_affinity_matrix, 0.0), axis=1),
        ),
        "fsdp",
    )
    own_totals = lax.dynamic_slice_in_dim(normalizer_sums, fsdp_index * strs, strs)
    own_positive = lax.dynamic_slice_in_dim(positive, fsdp_index * strs, strs)
    own_loss = jnp.sum(jnp.log(own_totals) - own_positive)
    affinity_derivative = (
        (
            exponentiated_affinity / normalizer_sums[:, None]
            - matching_pair_indicator.astype(jnp.float32)
        )
        / sharpness_divisor
    ).astype(jnp.bfloat16)
    picked = affinity_derivative
    row_part = lax.psum_scatter(
        jnp.dot(picked, cols, preferred_element_type=jnp.float32).astype(jnp.bfloat16),
        "fsdp",
        scatter_dimension=0,
        tiled=True,
    ).astype(jnp.float32)
    picked = affinity_derivative
    col_part = lax.psum_scatter(
        lax.dot_general(
            picked, sample_count, (((0,), (0,)), ((), ())), preferred_element_type=jnp.float32
        ).astype(jnp.bfloat16),
        "dp",
        scatter_dimension=0,
        tiled=True,
    ).astype(jnp.float32)
    grad_emb = row_part + col_part
    grad_pooled = (grad_emb - unit * jnp.sum(unit * grad_emb, axis=-1, keepdims=True)) / norm
    grad_split = grad_pooled.reshape(strs, KVH, groups, HD)
    grad_value = jnp.einsum("skgt,skgd->tkd", probs, grad_split, precision=highest).reshape(
        tok_rows, kv_width
    )
    up_part = lax.dot_general(low, grad_value, (((0,), (0,)), ((), ())), precision=highest)
    grad_low = lax.dot_general(
        grad_value, up_f, (((1,), (1,)), ((), ())), precision=highest
    ).astype(jnp.bfloat16)
    columns = hidden
    shard = lax.psum_scatter(
        lax.dot_general(
            columns, grad_low, (((0,), (0,)), ((), ())), preferred_element_type=jnp.float32
        ).astype(jnp.bfloat16),
        "fsdp",
        scatter_dimension=0,
        tiled=True,
    )
    down_grad = lax.psum(shard, "dp").astype(jnp.float32)
    up_grad, loss_sum = lax.psum((up_part, own_loss), ("dp", "fsdp"))
    loss = loss_sum / (strs * n_dp * n_fsdp)
    return (loss, down_grad, up_grad)


LANES = 128
MESH = pl.DeviceIdType.MESH
HIGHEST = lax.Precision.HIGHEST


def dot(x, y, cx, cy, precision=None):
    return lax.dot_general(
        x, y, (((cx,), (cy,)), ((), ())), precision=precision, preferred_element_type=jnp.float32
    )


def fits(hidden, keys, queries, value_weight, adapter_down, adapter_up, lengths, partner):
    n_dp, n_fsdp = lax.axis_size("dp"), lax.axis_size("fsdp")
    strings = n_dp * n_fsdp * queries.shape[0]
    rank, width = adapter_up.shape
    return (
        n_fsdp == 4
        and n_dp == 8
        and strings <= 1024
        and queries.shape[0] == 16
        and (rank // 16) * (width // LANES) == n_dp
        and hidden.shape[1] == n_dp * n_fsdp * LANES
    )


def fused(
    n_dp,
    hidden_hbm,
    keys_hbm,
    queries_hbm,
    weight_hbm,
    down_in_hbm,
    up_hbm,
    len_hbm,
    partner_hbm,
    loss_ref,
    down_ref,
    up_out_ref,
    hidden_ref,
    keys_ref,
    queries_ref,
    up_ref,
    len_ref,
    partner_ref,
    w_all,
    acc,
    low_t,
    probs,
    emb_all,
    unit_ref,
    totals,
    msg,
    got1,
    sum1,
    got2,
    sum2,
    got3,
    final,
    send_sem,
    w_sem,
    e_sem,
    g_sem,
    load_sem,
):
    f32, bf16 = jnp.float32, jnp.bfloat16
    a, f = lax.axis_index("dp"), lax.axis_index("fsdp")
    nz = n_dp // 2
    z, k = a // 2, a % 2
    other = 1 - k
    xn = f + 1 - 2 * (f % 2)
    yn = (f + 2) % 4
    dn = (xn + 2) % 4
    pair_dev = (z * 2 + other, f)
    x_dev, y_dev, d_dev = (a, xn), (a, yn), (a, dn)
    upper = z // 2
    inner = z + upper * (3 - 2 * z)
    z_list = [z] + [t + upper * (3 - 2 * t) for t in (1 - inner, 2, 3)]
    z_devs = [(zz * 2 + k, f) for zz in z_list]

    barrier = pltpu.get_barrier_semaphore()
    peers = [pair_dev, x_dev, y_dev, d_dev] + z_devs[1:]
    for dev in peers:
        pl.semaphore_signal(barrier, inc=1, device_id=dev, device_id_type=MESH)

    tok, strs = hidden_ref.shape[0], queries_ref.shape[0]
    rank, width = up_ref.shape
    emb_w = queries_ref.shape[1]
    groups = HEADS // KVH
    half = weight_hbm.shape[0] // 2
    tall = half + rank
    edge = tall // 4 // 16 * 16
    sizes = [edge, tall // 2 - edge, tall // 2 - edge, edge]
    offsets = [0, edge, tall // 2, tall - edge]
    strings = emb_all.shape[0]

    loads = []

    def load(src, dst):
        copy = pltpu.make_async_copy(src, dst, load_sem.at[len(loads)])
        copy.start()
        loads.append(copy)

    for h in range(2):
        load(weight_hbm.at[pl.ds(h * half, half), :], w_all.at[f, h, pl.ds(0, half), :])
        load(down_in_hbm.at[:, pl.ds(h * half, half)], w_all.at[f, h, pl.ds(half, rank), :])
    load(queries_hbm, queries_ref)
    load(keys_hbm, keys_ref)
    load(len_hbm, len_ref)
    load(partner_hbm, partner_ref)
    load(up_hbm, up_ref)
    load(hidden_hbm, hidden_ref)
    for copy in loads[:4]:
        copy.wait()
    pl.semaphore_wait(barrier, len(peers))

    sends = []

    def push(src, dst, recv, dev):
        copy = pltpu.make_async_remote_copy(
            src_ref=src,
            dst_ref=dst,
            send_sem=send_sem.at[len(sends)],
            recv_sem=recv,
            device_id=dev,
            device_id_type=MESH,
        )
        copy.start()
        sends.append(copy)

    drained = []

    def drain():
        for copy in sends[len(drained) :]:
            copy.wait_send()
            drained.append(copy)

    def arrive(dst, recv):
        pltpu.make_async_remote_copy(
            src_ref=dst,
            dst_ref=dst,
            send_sem=send_sem.at[0],
            recv_sem=recv,
            device_id=pair_dev,
            device_id_type=MESH,
        ).wait_recv()

    flip = z % 2
    z_dev = ((z + 1 - 2 * flip) * 2 + k, f)

    def w_slot(s, h, q):
        start = offsets[q] + flip * (offsets[3 - q] - offsets[q])
        here = pl.ds(pl.multiple_of(start, 16), sizes[q])
        return w_all.at[s, h, here, :], w_sem.at[s, h, q + flip * (3 - 2 * q)]

    def w_push(s, q, dev):
        ref, sem = w_slot(s, k, q)
        push(ref, ref, sem, dev)

    def w_arrive(s, h, q):
        arrive(*w_slot(s, h, q))

    for q in range(2):
        w_push(f, q, x_dev)
        w_push(f, 1 - q, y_dev)
    for copy in loads[4:]:
        copy.wait()

    rows = groups * strs
    row_str = lax.broadcasted_iota(jnp.int32, (rows, strs), 0) % strs
    lane_str = lax.broadcasted_iota(jnp.int32, (rows, strs), 1)
    len_f = jnp.broadcast_to(len_ref[...].astype(f32), (rows, strs))
    ends = jnp.sum(jnp.where(lane_str <= row_str, len_f, 0.0), axis=1, keepdims=True)
    starts = jnp.sum(jnp.where(lane_str < row_str, len_f, 0.0), axis=1, keepdims=True)
    at = lax.broadcasted_iota(jnp.int32, (rows, tok), 1).astype(f32)
    member = (at >= starts) & (at < ends)
    for kv in range(KVH):
        q = jnp.concatenate(
            [
                queries_ref[:, (kv * groups + g) * HD : (kv * groups + g + 1) * HD]
                for g in range(groups)
            ],
            axis=0,
        )
        scores = dot(q, keys_ref[:, kv * HD : (kv + 1) * HD], 1, 1) / math.sqrt(HD)
        raw = jnp.where(member, jnp.exp(scores), 0.0)
        probs[kv] = raw / jnp.sum(raw, axis=1, keepdims=True)

    acc[...] = jnp.zeros_like(acc)
    low_t[...] = jnp.zeros_like(low_t)

    def project(s, h):
        x = hidden_ref[:, pl.ds(pl.multiple_of((2 * s + h) * half, half), half)]
        acc[...] += dot(x, w_all[s, h, 0:half, :], 1, 0)
        low_t[...] += dot(w_all[s, h, half : half + rank, :], x, 1, 1)

    project(f, 0)
    project(f, 1)
    def w_relay(s, q, on):
        w_arrive(s, k, q)
        for dev in on:
            w_push(s, q, dev)
        w_push(s, q, pair_dev)

    w_relay(xn, 0, (y_dev, z_dev))
    w_relay(yn, 1, (x_dev,))
    w_push(f, 2, x_dev)
    w_push(f, 2, y_dev)
    w_relay(yn, 0, (z_dev,))
    w_relay(xn, 1, ())
    w_relay(dn, 0, (z_dev,))
    w_relay(dn, 1, (z_dev,))
    for q in (3, 2):
        w_relay(xn, q, ())
        w_relay(yn, q, ())
    project(xn, k)
    project(yn, k)
    for s in (xn, yn):
        for q in range(4):
            w_arrive(s, other, q)
        project(s, other)
    for q in (3, 2):
        w_relay(dn, q, ())
    project(dn, k)
    for q in range(4):
        w_arrive(dn, other, q)
    project(dn, other)
    up_f = up_ref[...].astype(f32)
    value = acc[...] + dot(low_t[...], up_f, 0, 0, HIGHEST)
    square = jnp.zeros((strs, 1), f32)
    for kv in range(KVH):
        pooled = dot(probs[kv], value[:, kv * HD : (kv + 1) * HD], 1, 0, HIGHEST)
        for g in range(groups):
            part = pooled[g * strs : (g + 1) * strs, :]
            unit_ref[:, (kv * groups + g) * HD : (kv * groups + g + 1) * HD] = part
            square += jnp.sum(part * part, axis=1, keepdims=True)
    norm = jnp.sqrt(square + 1e-06)
    unit = unit_ref[...] / norm
    unit_ref[...] = unit
    emb = unit.astype(bf16)

    def block_of(zz, kk, ff):
        d = (zz * 2 + kk) * 4 + ff
        return emb_all.at[pl.ds(pl.multiple_of(d * strs, strs), strs), :], e_sem.at[d]

    mine = (a * 4 + f) * strs
    own_rows = pl.ds(pl.multiple_of(mine, strs), strs)
    emb_all[own_rows, 0:emb_w] = emb
    partner_row = partner_ref[...].astype(f32)
    own_partner = jnp.sum(
        jnp.where(
            lax.broadcasted_iota(jnp.int32, (strs, strs), 0)
            == lax.broadcasted_iota(jnp.int32, (strs, strs), 1),
            jnp.broadcast_to(partner_row, (strs, strs)),
            0.0,
        ),
        axis=1,
        keepdims=True,
    )
    high = jnp.floor(own_partner * (1.0 / 256.0))
    lane = lax.broadcasted_iota(jnp.int32, (strs, LANES), 1)
    emb_all[own_rows, emb_w : emb_w + LANES] = jnp.where(
        lane == 0, own_partner - 256.0 * high, jnp.where(lane == 1, high, 0.0)
    ).astype(bf16)

    def e_push(blk, dev):
        push(blk[0], blk[0], blk[1], dev)

    own_block = block_of(z, k, f)
    for dev in z_devs[1:]:
        e_push(own_block, dev)
    for dev in (x_dev, y_dev, pair_dev):
        e_push(own_block, dev)
    drain()

    def from_z(r, devs):
        blk = block_of(z_list[r], k, f)
        arrive(*blk)
        for dev in devs:
            e_push(blk, dev)

    def from_plane(r):
        for s, relay in ((xn, y_dev), (yn, x_dev)):
            blk = block_of(z_list[r], k, s)
            arrive(*blk)
            if r < nz - 1 and (r % 2 == 0) == (s is xn):
                e_push(blk, relay)
            e_push(blk, pair_dev)

    from_z(1, (x_dev, y_dev, pair_dev))
    from_plane(0)
    from_z(2, (x_dev, y_dev, pair_dev))
    from_plane(1)
    from_z(3, (d_dev, x_dev, y_dev, pair_dev))
    from_plane(2)
    from_plane(3)
    for r in range(nz):
        blk = block_of(z_list[r], k, dn)
        arrive(*blk)
        e_push(blk, pair_dev)
    for r in range(nz):
        for s in (f, xn, yn, dn):
            arrive(*block_of(z_list[r], other, s))

    step = min(strings, 128)

    def rows_of(i, loss):
        here = pl.ds(pl.multiple_of(i * step, step), step)
        logits = dot(emb_all[here, 0:emb_w], emb_all[:, 0:emb_w], 1, 1) * (1.0 / sharpness_divisor)
        row = i * step + lax.broadcasted_iota(jnp.int32, (step, strings), 0)
        col = lax.broadcasted_iota(jnp.int32, (step, strings), 1)
        total = jnp.sum(jnp.where(row != col, jnp.exp(logits), 0.0), axis=1, keepdims=True)
        totals[here, :] = jnp.broadcast_to(total, (step, LANES))
        code = emb_all[here, emb_w : emb_w + LANES].astype(f32)
        mate = code[:, 0:1] + 256.0 * code[:, 1:2]
        positive = jnp.sum(
            jnp.where(mate == col.astype(f32), logits, 0.0), axis=1, keepdims=True
        )
        return loss + jnp.sum(jnp.log(total) - positive, axis=0, keepdims=True)

    loss = lax.fori_loop(0, strings // step, rows_of, jnp.zeros((1, 1), f32))
    loss_ref[...] = jnp.broadcast_to(loss / strings, loss_ref.shape)

    logits = dot(emb_all[:, 0:emb_w], emb, 1, 1) * (1.0 / sharpness_divisor)
    j = lax.broadcasted_iota(jnp.int32, (strings, strs), 0)
    i = mine + lax.broadcasted_iota(jnp.int32, (strings, strs), 1)
    expd = jnp.where(i != j, jnp.exp(logits), 0.0)
    own_total = jnp.sum(expd, axis=0, keepdims=True)
    own_hit = jnp.where(partner_row == j.astype(f32), 1.0, 0.0)
    code = emb_all[:, emb_w : emb_w + LANES].astype(f32)
    mate = code[:, 0:1] + 256.0 * code[:, 1:2]
    hit = jnp.where(mate == i.astype(f32), 1.0, 0.0)
    row_grad = ((expd / own_total - own_hit) * (1.0 / sharpness_divisor)).astype(bf16)
    col_grad = ((expd / totals[:, 0:1] - hit) * (1.0 / sharpness_divisor)).astype(bf16)
    every = emb_all[:, 0:emb_w]
    grad_emb = dot(row_grad, every, 0, 0) + dot(col_grad, every, 0, 0)
    unit = unit_ref[...]
    grad_pooled = (grad_emb - unit * jnp.sum(unit * grad_emb, axis=1, keepdims=True)) / norm

    for kv in range(KVH):
        g_kv = jnp.concatenate(
            [
                grad_pooled[:, (kv * groups + g) * HD : (kv * groups + g + 1) * HD]
                for g in range(groups)
            ],
            axis=0,
        )
        acc[:, kv * HD : (kv + 1) * HD] = dot(
            probs[kv].astype(bf16), g_kv.astype(bf16), 0, 0
        )
    grad_value = acc[...].astype(bf16)
    up_part = dot(low_t[...].astype(bf16), grad_value, 1, 0).astype(bf16)
    grad_low_t = dot(up_ref[...], grad_value, 1, 1).astype(bf16)

    per_row = width // LANES
    span = n_dp * LANES
    for ff in range(4):
        part = dot(grad_low_t, hidden_ref[:, ff * span : (ff + 1) * span], 1, 0).astype(bf16)
        for aa in range(n_dp):
            msg[aa % 2, ff, aa // 2, 0:rank, :] = part[:, aa * LANES : (aa + 1) * LANES]
            r0, c0 = aa // per_row * 16, aa % per_row * LANES
            msg[aa % 2, ff, aa // 2, rank : rank + 16, :] = up_part[r0 : r0 + 16, c0 : c0 + LANES]

    push(msg.at[other], got1, g_sem.at[0], pair_dev)
    drain()
    arrive(got1, g_sem.at[0])
    sum1[...] = (msg[k].astype(f32) + got1[...].astype(f32)).astype(bf16)
    for n, (s, dev) in enumerate(((xn, x_dev), (yn, y_dev), (dn, d_dev))):
        push(sum1.at[s], got2.at[f], g_sem.at[1 + f], dev)
    got2[f] = sum1[f]
    for s in (xn, yn, dn):
        arrive(got2.at[s], g_sem.at[1 + s])
    total2 = got2[0].astype(f32)
    for s in range(1, 4):
        total2 += got2[s].astype(f32)
    sum2[...] = total2.astype(bf16)
    for r in range(1, nz):
        push(sum2.at[z_list[r]], got3.at[z], g_sem.at[5 + z], z_devs[r])
    got3[z] = sum2[z]
    for r in range(1, nz):
        arrive(got3.at[z_list[r]], g_sem.at[5 + z_list[r]])
    total3 = got3[0].astype(f32)
    for s in range(1, nz):
        total3 += got3[s].astype(f32)
    final[k, z] = total3.astype(bf16)
    fin = final.at[k, z]
    base = 5 + nz
    for dev in z_devs[1:] + [pair_dev]:
        push(fin, fin, g_sem.at[base + a], dev)
    for r in range(1, nz):
        slot, sem = final.at[k, z_list[r]], g_sem.at[base + z_list[r] * 2 + k]
        arrive(slot, sem)
        push(slot, slot, sem, pair_dev)
    for r in range(nz):
        arrive(final.at[other, z_list[r]], g_sem.at[base + z_list[r] * 2 + other])
    for aa in range(n_dp):
        r0, c0 = aa // per_row * 16, aa % per_row * LANES
        down_ref[:, aa * LANES : (aa + 1) * LANES] = final[aa % 2, aa // 2, 0:rank, :].astype(f32)
        up_out_ref[r0 : r0 + 16, c0 : c0 + LANES] = final[
            aa % 2, aa // 2, rank : rank + 16, :
        ].astype(f32)
    drain()


def fused_shards(hidden, keys, queries, value_weight, adapter_down, adapter_up, lengths, partner):
    n_dp, n_fsdp = lax.axis_size("dp"), lax.axis_size("fsdp")
    tok, depth = hidden.shape
    strs, emb_w = queries.shape
    shard, width = value_weight.shape
    rank = adapter_up.shape[0]
    nz = n_dp // 2
    strings = n_dp * n_fsdp * strs
    f32, bf16 = jnp.float32, jnp.bfloat16
    tall = rank + 16
    vmem = pl.BlockSpec(memory_space=pltpu.VMEM)
    hbm = pl.BlockSpec(memory_space=pltpu.HBM)
    blocks = n_dp * n_fsdp
    loss, down_t, up_grad = pl.pallas_call(
        functools.partial(fused, n_dp),
        out_shape=(
            jax.ShapeDtypeStruct((1, 1), f32),
            jax.ShapeDtypeStruct((rank, shard), f32),
            jax.ShapeDtypeStruct((rank, width), f32),
        ),
        in_specs=[hbm] * 8,
        out_specs=(vmem,) * 3,
        scratch_shapes=[
            pltpu.VMEM(hidden.shape, bf16),
            pltpu.VMEM(keys.shape, bf16),
            pltpu.VMEM(queries.shape, bf16),
            pltpu.VMEM(adapter_up.shape, bf16),
            pltpu.VMEM((1, strs), jnp.int32),
            pltpu.VMEM((1, strs), jnp.int32),
            pltpu.VMEM((n_fsdp, 2, shard // 2 + rank, width), bf16),
            pltpu.VMEM((tok, width), f32),
            pltpu.VMEM((rank, tok), f32),
            pltpu.VMEM((KVH, strs * HEADS // KVH, tok), f32),
            pltpu.VMEM((strings, emb_w + LANES), bf16),
            pltpu.VMEM((strs, emb_w), f32),
            pltpu.VMEM((strings, LANES), f32),
            pltpu.VMEM((2, n_fsdp, nz, tall, LANES), bf16),
            pltpu.VMEM((n_fsdp, nz, tall, LANES), bf16),
            pltpu.VMEM((n_fsdp, nz, tall, LANES), bf16),
            pltpu.VMEM((n_fsdp, nz, tall, LANES), bf16),
            pltpu.VMEM((nz, tall, LANES), bf16),
            pltpu.VMEM((nz, tall, LANES), bf16),
            pltpu.VMEM((2, nz, tall, LANES), bf16),
            pltpu.SemaphoreType.DMA((64 + 4 * n_dp,)),
            pltpu.SemaphoreType.DMA((n_fsdp, 2, 4)),
            pltpu.SemaphoreType.DMA((blocks,)),
            pltpu.SemaphoreType.DMA((5 + nz + n_dp,)),
            pltpu.SemaphoreType.DMA((10,)),
        ],
        compiler_params=pltpu.CompilerParams(
            collective_id=0, has_side_effects=True, vmem_limit_bytes=63 * 1024 * 1024
        ),
    )(
        hidden,
        keys,
        queries,
        value_weight,
        adapter_down.T,
        adapter_up,
        lengths,
        partner.reshape(1, strs),
    )
    return (loss[0, 0], down_t.T, up_grad)


def solution(mesh):
    placed = (
        P(("dp", "fsdp"), None),
        P(("dp", "fsdp"), None),
        P(("dp", "fsdp"), None),
        P("fsdp", None),
        P("fsdp", None),
        P(),
        P(("dp", "fsdp"), None),
        P(("dp", "fsdp")),
    )

    def body(*args):
        return (fused_shards if fits(*args) else shards)(*args)

    return jax.shard_map(
        body, mesh=mesh, in_specs=placed, out_specs=(P(), P("fsdp", None), P()), check_vma=False
    )
```
